32 devices in a mesh: grp: 2 (over x), gx: 16 (over z, y, core).
Axes of the slice: x: 2, y: 2, z: 4, core: 2. Of those that a mesh axis runs over, the one named last changes fastest.
Arguments:
- rhs: float32 [640, 12800], P(('grp', 'gx')), parts along dimension 0, may hold values from -4 to 4
- accumulation: bfloat16 [640, 12800], P(('grp', 'gx')), parts along dimension 0, may hold values from 0.0099487305 to 0.099609375
- trans_x: bfloat16 [640, 12800], P(('grp', 'gx')), parts along dimension 0, may hold values from 0.049804688 to 1
- trans_y: bfloat16 [640, 12800], P(('grp', 'gx')), parts along dimension 0, may hold values from 0.049804688 to 1
- trans_z: bfloat16 [640, 12800], P(('grp', 'gx')), parts along dimension 0, may hold values from 0.049804688 to 1
- basis_center: bfloat16 [640, 12800], P(('grp', 'gx')), parts along dimension 0, may hold values from 0.5 to 1
- basis_side: bfloat16 [2, 640, 12800], P(None, ('grp', 'gx')), parts along dimension 1, may hold values from 0 to 0.5
- coarse_inverse: float32 [64, 128], P(('grp', 'gx')), parts along dimension 0, may hold values from 0.001 to 0.004
Outputs:
- correction: float32 [640, 12800], P(('grp', 'gx')), parts along dimension 0
- coarse_update: float32 [64, 128], P(('grp', 'gx')), parts along dimension 0
The draws below stay inside these ranges and needn't reach their ends.
There are 2 independent parts, one for each index of `grp`. The reference program is written for one: setup_inputs(seed, part) draws one part's arguments, and reference() takes and returns one part's arrays. A program takes and returns all parts, laid end to end along the dimension named above; each array names one. Nothing has to cross between parts.
All inputs are finite; a program needn't handle non-finite values.
Results may differ from the reference program's by a relative error of at most 0.0003.
Values may be sent and summed in bfloat16 or wider, within the bound.
No kernel may reach another device: no remote copies, remote signals or barrier semaphores. Data moves between devices by JAX's collectives and lax.ppermute only.
A program may use at most 64 MiB of HBM per device.

```python
import math
import jax
import jax.numpy as jnp

BLK = 10
NCY = 8
NCZ = 16
PRE = 3
CSW = 6
POST = 3
NZ = 160
PLANE = 12800
COARSE = 128
NX = 320
NCX = 32


def draw_rhs(key, part):
    key = jax.random.fold_in(key, 11)
    rough_key, block_key = jax.random.split(key)
    rough_part = 0.8 * jnp.clip(jax.random.normal(rough_key, (NX, PLANE), jnp.float32), -3.0, 3.0)
    levels = 0.6 * jnp.clip(jax.random.normal(block_key, (NCX, NCY, NCZ), jnp.float32), -2.5, 2.5)
    grid_field = jnp.broadcast_to(levels[:, None, :, None, :, None], (NCX, BLK, NCY, BLK, NCZ, BLK)).reshape(NX, PLANE)
    return (rough_part + grid_field).astype(jnp.float32)


def level_of(own_key, dims, cuts, least, high):
    gain, own = 1.0, jax.random.fold_in(own_key, 6)
    for axis_at, shards_of in cuts:
        draws = jnp.exp(jax.random.uniform(jax.random.fold_in(own, axis_at), (shards_of,), jnp.float32, least / len(cuts), high / len(cuts)))
        gain = gain * jnp.repeat(draws, dims[axis_at] // shards_of).reshape([-1 if axis == axis_at else 1 for axis in range(len(dims))])
    return gain


def setup_inputs(seed: int = 0, part: int = 0) -> dict:
    splits = jax.random.split(jax.random.key(seed), 9)
    part_keys = jax.random.split(jax.random.fold_in(splits[8], part), 9)
    rhs = draw_rhs(jax.random.fold_in(jax.random.fold_in(splits[8], part), 71), part)
    accumulation = jnp.clip(jnp.exp(math.log(0.099609375) - 2.3038113 * jax.random.uniform(part_keys[1], (NX, PLANE), jnp.float32) ** level_of(part_keys[1], (NX, PLANE), ((0, 16),), -0.2, 0.2)), 0.0099487305, 0.099609375).astype(jnp.bfloat16)
    trans_x = jnp.clip(jnp.exp(math.log(1.0) - 2.9996462 * jax.random.uniform(part_keys[2], (NX, PLANE), jnp.float32) ** level_of(part_keys[2], (NX, PLANE), ((0, 16),), -0.2, 0.2)), 0.049804688, 1.0).astype(jnp.bfloat16)
    trans_y = jnp.clip(jnp.exp(math.log(1.0) - 2.9996462 * jax.random.uniform(part_keys[3], (NX, PLANE), jnp.float32) ** level_of(part_keys[3], (NX, PLANE), ((0, 16),), -0.2, 0.2)), 0.049804688, 1.0).astype(jnp.bfloat16)
    trans_z = jnp.clip(jnp.exp(math.log(1.0) - 2.9996462 * jax.random.uniform(part_keys[4], (NX, PLANE), jnp.float32) ** level_of(part_keys[4], (NX, PLANE), ((0, 16),), -0.2, 0.2)), 0.049804688, 1.0).astype(jnp.bfloat16)
    basis_center = jnp.clip(0.5 + 0.5 * jax.random.uniform(part_keys[5], (NX, PLANE), jnp.float32) ** level_of(part_keys[5], (NX, PLANE), ((0, 16),), -0.2, 0.2), 0.5, 1.0).astype(jnp.bfloat16)
    basis_side = jnp.clip(0.5 * jax.random.uniform(part_keys[6], (2, NX, PLANE), jnp.float32) ** level_of(part_keys[6], (2, NX, PLANE), ((1, 16),), -0.2, 0.2), 0.0, 0.5).astype(jnp.bfloat16)
    coarse_inverse = jnp.clip(jnp.exp(math.log(0.004) - 1.3862944 * jax.random.uniform(part_keys[7], (NCX, COARSE), jnp.float32) ** level_of(part_keys[7], (NCX, COARSE), ((0, 16),), -0.2, 0.2)), 0.001, 0.004)
    return {"rhs": rhs, "accumulation": accumulation, "trans_x": trans_x, "trans_y": trans_y, "trans_z": trans_z, "basis_center": basis_center, "basis_side": basis_side, "coarse_inverse": coarse_inverse}


OMEGA_FINE = 0.7
OMEGA_COARSE = 0.6


def yz_terms(field, trans_y, trans_yp, trans_z, trans_zp, upper_z):
    y_up = jnp.pad(field, ((0, 0), (0, NZ)))[:, NZ:]
    y_down = jnp.pad(field, ((0, 0), (NZ, 0)))[:, :-NZ]
    z_up = jnp.pad(field, ((0, 0), (0, 1)))[:, 1:] * upper_z
    z_down = jnp.pad(field, ((0, 0), (1, 0)))[:, :-1]
    return trans_y * (field - y_up) + trans_yp * (field - y_down) + trans_z * (field - z_up) + trans_zp * (field - z_down)


def operate(padded, coeffs):
    accum, trans_xf, trans_xp, trans_yf, trans_yp, trans_zf, trans_zp, upper_z = coeffs
    field = padded[1:-1]
    out = accum * field + trans_xf * (field - padded[2:]) + trans_xp * (field - padded[:-2])
    return out + yz_terms(field, trans_yf, trans_yp, trans_zf, trans_zp, upper_z)


def block_sum(field):
    return field.reshape(NCX, BLK, NCY, BLK, NCZ, BLK).sum(axis=(1, 3, 5)).reshape(NCX, COARSE)


def expand(coarse):
    count = coarse.shape[0]
    grid = jnp.broadcast_to(coarse.reshape(count, NCY, 1, NCZ, 1), (count, NCY, BLK, NCZ, BLK))
    return grid.reshape(count, PLANE)


def reference(rhs, accumulation, trans_x, trans_y, trans_z, basis_center, basis_side, coarse_inverse):
    f32 = jnp.float32
    zpos = jnp.arange(PLANE, dtype=jnp.int32) % NZ
    upper_z = (zpos != NZ - 1).astype(f32)[None]
    lower_z = (zpos != 0).astype(f32)[None]
    accum = accumulation.astype(f32)
    trans_xf = trans_x.astype(f32)
    trans_yf = trans_y.astype(f32)
    trans_zf = trans_z.astype(f32)
    trans_xp = jnp.pad(trans_xf, ((1, 0), (0, 0)))[:-1]
    trans_yp = jnp.pad(trans_yf, ((0, 0), (NZ, 0)))[:, :-NZ]
    trans_zp = jnp.pad(trans_zf, ((0, 0), (1, 0)))[:, :-1] * lower_z
    coeffs = (accum, trans_xf, trans_xp, trans_yf, trans_yp, trans_zf, trans_zp, upper_z)
    diag = accum + trans_xf + trans_xp + trans_yf + trans_yp + trans_zf + trans_zp
    center = basis_center.astype(f32)
    side_lo = basis_side[0].astype(f32)
    side_hi = basis_side[1].astype(f32)

    def apply_a(field):
        return operate(jnp.pad(field, ((1, 1), (0, 0))), coeffs)

    def restrict(field):
        summed_c = block_sum(center * field)
        summed_lo = block_sum(side_lo * field)
        summed_hi = block_sum(side_hi * field)
        return summed_c + jnp.pad(summed_hi, ((1, 0), (0, 0)))[:-1] + jnp.pad(summed_lo, ((0, 1), (0, 0)))[1:]

    def prolong(coarse):
        spread = expand(jnp.pad(coarse, ((1, 1), (0, 0))))
        out = center.reshape(NCX, BLK, PLANE) * spread[1:-1, None] + side_lo.reshape(NCX, BLK, PLANE) * spread[:-2, None] + side_hi.reshape(NCX, BLK, PLANE) * spread[2:, None]
        return out.reshape(NX, PLANE)

    smooth = jnp.zeros((NX, PLANE), f32)
    for sweep_index in range(PRE):
        smooth = smooth + OMEGA_FINE * (rhs - apply_a(smooth)) / diag
    coarse_rhs = restrict(rhs - apply_a(smooth))
    coarse_update = jnp.zeros((NCX, COARSE), f32)
    for sweep_index in range(CSW):
        coarse_update = coarse_update + OMEGA_COARSE * coarse_inverse * (coarse_rhs - restrict(apply_a(prolong(coarse_update))))
    correction = smooth + prolong(coarse_update)
    for sweep_index in range(POST):
        correction = correction + OMEGA_FINE * (rhs - apply_a(correction)) / diag
    return correction, coarse_update
```

```python
import jax
import jax.numpy as jnp
from jax import lax
from jax.experimental import pallas as pl
from jax.experimental.pallas import tpu as pltpu
from jax.sharding import PartitionSpec as P

BLK = 10
NCY = 8
NCZ = 16
CSW = 6
NZ = 160
PLANE = 12800
COARSE = NCY * NCZ
OMEGA_FINE = 0.7
OMEGA_COARSE = 0.6

LANES = 128
TILES = PLANE // LANES
PHASES = 5
PAIR = 25
PAIRS = TILES // PAIR
OWN = 20
TOP = 8
PAD = 32
GROUP = 20
QUARTERS = 4
LT = QUARTERS * NZ // LANES
PAIRED = ((0, 0), (0, 1), (0, 2), (1, 1), (1, 2), (2, 2))
PLANES = 16
WHOLE = TILES // 16
REST = TILES % 16
OFFSET = (0, -1, 1)
SAME = ((0, 0), (0, 1), (0, 2), (0, 3), (1, 1), (1, 2), (1, 3), (2, 2), (2, 3), (3, 3), (1, 4), (2, 4), (3, 4))
ACROSS = tuple((u, v) for u in range(4) for v in range(4) if abs(u - v) <= 2)
Y_ROW = len(SAME)
Z_ROW = Y_ROW + len(ACROSS)
INVERSE_ROW = Z_ROW + len(ACROSS)
RHS_ROW = INVERSE_ROW + 2
ALL_ROWS = 48
F32 = jnp.float32
BF16 = jnp.bfloat16


def params(mib):
    return pltpu.CompilerParams(vmem_limit_bytes=mib << 20)


def vmem(shape, dtype=F32):
    return pltpu.VMEM(shape, dtype)


def in_vmem(count):
    return [pl.BlockSpec(memory_space=pltpu.VMEM)] * count


def in_hbm(count):
    return [pl.BlockSpec(memory_space=pltpu.HBM)] * count


def padded():
    return vmem((TILES * PAD, LANES))


def padded_out():
    return pltpu.HBM((TILES * PAD, LANES), F32)


def cells(dtype=BF16):
    return vmem((OWN, PLANE), dtype)


def semaphores(*shape):
    return pltpu.SemaphoreType.DMA(shape)


def stream(sources, buffers, sems):
    width = PLANE // PAIRS

    def copy(field, n):
        lanes = pl.ds(pl.multiple_of(n * width, width), width)
        return pltpu.make_async_copy(
            sources[field].at[:, lanes], buffers[field].at[:, lanes], sems.at[field, n]
        )

    for n in range(PAIRS):
        for field in range(len(sources)):
            copy(field, n).start()

    def wait(n):
        for field in range(len(sources)):
            copy(field, n).wait()

    return wait


def copies(sources, targets, sems):
    made = [
        pltpu.make_async_copy(src, dst, sems.at[n])
        for n, (src, dst) in enumerate(zip(sources, targets))
    ]
    for copy in made:
        copy.start()
    return made


def lane_roll(value, steps):
    return pltpu.roll(value, steps % LANES, 1)


def lanes_of(rows):
    return lax.broadcasted_iota(jnp.int32, (rows, LANES), 1)


def rows_of(rows):
    return lax.broadcasted_iota(jnp.int32, (rows, LANES), 0)


def at(t):
    return pl.ds(pl.multiple_of(t * LANES, LANES), LANES)


def span(t, low, count):
    return pl.ds(t * PAD + low, count)


def own(ref, t):
    return ref[:, at(t)].astype(F32)


def over_tiles(body, carry, before=None, unroll=1):
    def step(n, carry):
        if before is not None:
            before(n)
        for i in range(PAIR):
            carry = body(n * PAIR + i, i, carry)
        return carry

    return lax.fori_loop(0, PAIRS, step, carry, unroll=unroll)


def halves(value):
    high = value.astype(BF16)
    low = (value - high.astype(F32)).astype(BF16)
    return high, low


def remainder(value):
    return value - value.astype(BF16).astype(F32)


def parity():
    return lax.rem(lax.axis_index("gx"), 2)


def coupled(src, tx, ty, tz, t, low, count, carry):
    center, following, y_next, z_flux, y_flux, y_flux_before = carry
    lane = lanes_of(count)
    here = span(t, low, count)
    second = src[span(jnp.minimum(t + 2, TILES - 1), low, count), :]
    z_up = jnp.where(lane == LANES - 1, lane_roll(following, -1), lane_roll(center, -1))
    y_second = lane_roll(second, -(NZ - LANES))
    y_up = jnp.where(lane >= 2 * LANES - NZ, y_second, y_next)
    tz_t = tz[here, :]
    ty_t = ty[here, :]
    z_flux_new = lane_roll(tz_t * center, 1)
    z_down = jnp.where(lane == 0, z_flux, z_flux_new)
    y_down = jnp.where(lane < NZ - LANES, y_flux_before, y_flux)
    y_flux_new = lane_roll(ty_t * center, NZ - LANES)
    total = tz_t * z_up + z_down
    total = total + (ty_t * y_up + y_down)
    total = total + tx[here, :] * src[span(t, low + 1, count), :]
    total = total + tx[span(t, low - 1, count), :] * src[span(t, low - 1, count), :]
    return total, (following, second, y_second, z_flux_new, y_flux_new, y_flux)


def coupled_start(src, low, count):
    center = src[span(0, low, count), :]
    following = src[span(1, low, count), :]
    zero = center * 0.0
    return center, following, lane_roll(following, -(NZ - LANES)), zero, zero, zero


def sweep(src, dst, tx, ty, tz, k, b, low, count):
    def body(t, i, carry):
        total, after = coupled(src, tx, ty, tz, t, low, count, carry)
        here = span(t, low, count)
        dst[here, :] = b[here, :] + (1.0 - OMEGA_FINE) * carry[0] + k[here, :] * total
        return after

    over_tiles(body, coupled_start(src, low, count), unroll=2)


def plane(ref, row, q, size, stride=PAD):
    return pl.ds(16 * q * stride + row, size, stride)


def read_plane(ref, row, stride=PAD):
    return lambda q, size: ref[plane(ref, row, q, size, stride), :]


def send_both(pay_a, pay_b, tail_a, tail_b, right, left):
    even = parity() == 0
    for n in range(PLANES):
        for q in range(WHOLE + 1):
            size = 16 if q < WHOLE else REST
            r, l = right[n](q, size), left[n](q, size)
            a, b = jnp.where(even, r, l), jnp.where(even, l, r)
            if q < WHOLE:
                rows = slice((n * WHOLE + q) * 16, (n * WHOLE + q) * 16 + 16)
                pay_a[rows, :] = a.astype(BF16)
                pay_b[rows, :] = b.astype(BF16)
            else:
                rows = slice(n * REST, n * REST + REST)
                tail_a[rows, :] = a
                tail_b[rows, :] = b
    pay_a[PLANES * WHOLE * 16 :, :] = tail_a[...].astype(BF16)
    pay_b[PLANES * WHOLE * 16 :, :] = tail_b[...].astype(BF16)


def received(got_a, got_b, tail_a, tail_b):
    even = parity() == 0
    tail_a[...] = got_a[PLANES * WHOLE * 16 :, :].astype(F32)
    tail_b[...] = got_b[PLANES * WHOLE * 16 :, :].astype(F32)

    def both(n, q):
        if q < WHOLE:
            rows = slice((n * WHOLE + q) * 16, (n * WHOLE + q) * 16 + 16)
            a, b = got_a[rows, :].astype(F32), got_b[rows, :].astype(F32)
        else:
            rows = slice(n * REST, n * REST + REST)
            a, b = tail_a[rows, :], tail_b[rows, :]
        return jnp.where(even, b, a), jnp.where(even, a, b)

    return both


def payload():
    return jax.ShapeDtypeStruct((PLANES * TILES, LANES), BF16)


def tails():
    return [vmem((PLANES * REST, LANES))] * 2


def prepare_kernel(
    rhs, accum, trans_x, trans_y, trans_z, center, first_side, pay_a, pay_b,
    rhs_v, accum_v, x_v, y_v, z_v, center_v, raw, tx, ty, tz, dg, basis, tail_a, tail_b, sems,
):
    wait = stream(
        (rhs, accum, trans_x, trans_y, trans_z, center.at[0:16, :]),
        (rhs_v, accum_v, x_v, y_v, z_v, center_v),
        sems,
    )
    lane = lanes_of(12)

    def ends(ref, t):
        value = own(ref, t)
        return jnp.concatenate([value[0:8], value[16:20]], axis=0)

    def body(t, i, carry):
        z_before, y_before, y_second = carry
        z_pos = (i * LANES + lane) % NZ
        cells = t * LANES + lane
        here = pl.ds(t * 24 + 8, 12)
        x, y, z = ends(x_v, t), ends(y_v, t), ends(z_v, t)
        y_inner = jnp.where(cells < PLANE - NZ, y, 0.0)
        z_inner = jnp.where(z_pos != NZ - 1, z, 0.0)
        z_rolled = lane_roll(z_inner, 1)
        y_rolled = lane_roll(y_inner, NZ - LANES)
        tx[pl.ds(t * 24, 8), :] = jnp.zeros((8, LANES), F32)
        tx[here, :] = x
        ty[here, :] = y_inner
        tz[here, :] = z_inner
        total = ends(accum_v, t) + x + tx[pl.ds(t * 24 + 7, 12), :]
        total = total + y + jnp.where(lane < NZ - LANES, y_second, y_before)
        total = total + z + jnp.where(lane == 0, z_before, z_rolled)
        dg[here, :] = total
        raw[here, :] = ends(rhs_v, t)
        basis[pl.ds(t * 8, 2), :] = first_side[:, at(t)].astype(F32)
        basis[pl.ds(t * 8 + 2, 1), :] = center_v[:, at(t)].astype(F32)[0:1]
        return z_rolled, y_rolled, y_before

    zero = lanes_of(12).astype(F32) * 0.0
    over_tiles(body, (zero, zero, zero), wait)

    def low_part(f):
        return lambda q, size: remainder(f(q, size))

    def first_sweep(row):
        r, d = read_plane(raw, row, 24), read_plane(dg, row, 24)
        return lambda q, size: OMEGA_FINE * r(q, size) / d(q, size)

    def planes(near, second, far, x_rows):
        r, d = read_plane(raw, near, 24), read_plane(dg, near, 24)
        return (
            [r, low_part(r), read_plane(raw, second, 24)]
            + [d, low_part(d), read_plane(dg, second, 24)]
            + [read_plane(ref, row, 24) for ref in (ty, tz) for row in (near, second)]
            + [first_sweep(far)]
            + [read_plane(tx, row, 24) for row in x_rows]
        )

    right = planes(19, 18, 17, (19, 18, 17))
    left = planes(8, 9, 10, (8, 9))
    weights = [read_plane(basis, row, 8) for row in (2, 0, 1)]
    send_both(pay_a, pay_b, tail_a, tail_b, right + weights[:2], left + weights)


def prepare(rhs, accum, trans_x, trans_y, trans_z, center, first_side):
    return pl.pallas_call(
        prepare_kernel,
        out_shape=(payload(),) * 2,
        in_specs=in_hbm(6) + in_vmem(1),
        out_specs=tuple(in_vmem(2)),
        scratch_shapes=[cells(F32)]
        + [cells()] * 4
        + [vmem((16, PLANE), BF16)]
        + [vmem((TILES * 24, LANES))] * 5
        + [vmem((TILES * 8, LANES))]
        + tails()
        + [semaphores(6, PAIRS)],
        compiler_params=params(58),
    )(rhs, accum, trans_x, trans_y, trans_z, center, first_side)


def add_share(shares, u, v, value):
    pair = (min(u, v), max(u, v))
    shares[pair] = shares[pair] + value if pair in shares else value


def add_face(shares, u, v, value):
    add_share(shares, u, v, -2.0 * value if u == v else -value)


def presmooth_kernel(
    got_a, got_b, raw, tx_in, ty_in, tz_in, dg_in, w0, w1, w2, operator,
    tx, ty, tz, dg, tx_out, ty_out, tz_out, k_out, b_out, smooth_out, w0_out, w1_out, w2_out,
    part, pay_a, pay_b,
    k, b, smooth, work, sums, rest, edges, tail_a, tail_b, out_sems,
):
    weights = (w0, w1, w2)
    sent = copies(weights, (w0_out, w1_out, w2_out), out_sems.at[0:3])
    both = received(got_a, got_b, tail_a, tail_b)
    for q in range(WHOLE + 1):
        size = 16 if q < WHOLE else REST

        def put(ref, row, value):
            ref[plane(ref, row, q, size), :] = value

        def get(ref, row):
            return ref[plane(ref, row, q, size), :]

        values = [both(n, q) for n in range(PLANES)]
        left, right = [v[0] for v in values], [v[1] for v in values]
        for got, rows in ((left, (7, 6, 5)), (right, (28, 29, 30))):
            put(b, rows[0], got[0] + got[1])
            put(b, rows[1], got[2])
            put(dg, rows[1], got[5])
            put(ty, rows[0], got[6])
            put(ty, rows[1], got[7])
            put(tz, rows[0], got[8])
            put(tz, rows[1], got[9])
            put(b, rows[2], got[10])
            put(tx, rows[0], got[11])
            put(tx, rows[1], got[12])
        put(tx, 5, left[13])
        tx_before = left[11]
        tx_last = get(tx, TOP + OWN - 1)
        beyond = right[3] + right[4]
        put(dg, 7, left[3] + left[4])
        put(dg, 28, jnp.where(beyond > 0.0, beyond + tx_last, 0.0))
        put(dg, TOP, get(dg, TOP) + tx_before)
        first = [get(w, TOP) for w in weights]
        last = [get(w, TOP + OWN - 1) for w in weights]
        from_next = [right[13], right[14], right[15]]
        products = [tx_last * last[a] * from_next[c] for a in range(3) for c in range(3)]
        products += [tx_before * first[a] * first[c] for a, c in PAIRED]
        for n, value in enumerate(products):
            edges[plane(edges, n, q, size, 16), :] = value
        edges[plane(edges, 15, q, size, 16), :] = tx_last * 0.0

    sent += copies((tx, ty, tz), (tx_out, ty_out, tz_out), out_sems.at[3:6])

    def scale(t, i, carry):
        here = span(t, 6, 24)
        diag = dg[here, :]
        value = jnp.where(diag > 0.0, OMEGA_FINE / diag, 0.0)
        k[here, :] = value
        b[span(t, TOP, OWN), :] = raw[span(t, TOP, OWN), :]
        b[here, :] = value * b[here, :]
        return carry

    over_tiles(scale, 0)
    sent += copies((k, b), (k_out, b_out), out_sems.at[6:8])
    sweep(b, work, tx, ty, tz, k, b, 6, 24)
    sweep(work, smooth, tx, ty, tz, k, b, 7, 22)
    sent += copies((smooth,), (smooth_out,), out_sems.at[8:9])
    planes_r, planes_l = [], []
    for planes, rows in ((planes_r, (19, 18, 17)), (planes_l, (0, 1, 2))):
        for row in rows:
            f = read_plane(smooth, TOP + row)
            planes += [f, (lambda f: lambda q, size: remainder(f(q, size)))(f)]
        planes += [read_plane(w, TOP + row) for w in weights for row in rows]
        planes += [planes[-1]]
    send_both(pay_a, pay_b, tail_a, tail_b, planes_r, planes_l)

    sums[...] = jnp.zeros_like(sums)
    lane = lanes_of(64)
    row8 = rows_of(8)
    for n in range(PAIR):
        rest[n * 24 + 16 : n * 24 + 24, :] = jnp.zeros((8, LANES), F32)

    def residual(t, i, carry):
        total, following = coupled(smooth, tx, ty, tz, t, TOP, OWN, carry)
        rest[i * 24 : i * 24 + OWN, :] = (
            raw[span(t, TOP, OWN), :] - dg[span(t, TOP, OWN), :] * carry[0] + total
        )
        left_over = rest[i * 24 : i * 24 + 24, :]
        folded = []
        for w in weights:
            f = w[span(t, TOP, 24), :] * left_over
            mixed = jnp.where(row8 < BLK - 8, f[8:16], 0.0)
            folded += [f[0:8] + mixed, f[16:24] + (f[8:16] - mixed)]
        folded = jnp.concatenate(folded + [edges[pl.ds(t * 16, 16), :]], axis=0)
        n = t // PAIR
        phase = i % PHASES
        if i != PAIR // 2:
            sums[phase, 2 * n + (1 if i > PAIR // 2 else 0)] += folded
        else:
            sums[phase, 2 * n] += jnp.where(lane < LANES // 2, folded, 0.0)
            sums[phase, 2 * n + 1] += jnp.where(lane < LANES // 2, 0.0, folded)
        return following

    over_tiles(residual, coupled_start(smooth, TOP, OWN))

    src = lax.broadcasted_iota(jnp.int32, (LANES, LANES), 0)
    dst = lax.broadcasted_iota(jnp.int32, (LANES, LANES), 1)
    found = jnp.zeros((NCY * 64, LANES), F32)
    for phase in range(PHASES):
        pick = jnp.where((phase * LANES + src) % NZ // BLK == dst, 1.0, 0.0).astype(BF16)
        for piece in halves(sums[phase].reshape(NCY * 64, LANES)):
            found = found + jnp.dot(piece, pick, preferred_element_type=F32)
    placed = found[0:64]
    for strip in range(1, NCY):
        placed = placed + lane_roll(found[strip * 64 : strip * 64 + 64], strip * NCZ)
    shares = {}
    for n, (a, c) in enumerate(PAIRED):
        add_share(shares, 1 + OFFSET[a], 1 + OFFSET[c], placed[57 + n : 58 + n])
    for a in range(3):
        for c in range(3):
            add_face(shares, 2 + OFFSET[a], 3 + OFFSET[c], placed[48 + 3 * a + c : 49 + 3 * a + c])
    part[0:ALL_ROWS, :] = operator[...]
    for n, pair in enumerate(SAME):
        if pair in shares:
            part[n : n + 1, :] += shares[pair]
    for a in range(3):
        for block in range(2):
            row = RHS_ROW + 1 + block + OFFSET[a]
            low = (2 * a + block) * 8
            part[row : row + 1, :] += jnp.sum(placed[low : low + 8], axis=0, keepdims=True)
    for n in range(1, part.shape[0] // ALL_ROWS):
        part[n * ALL_ROWS : n * ALL_ROWS + ALL_ROWS, :] = part[0:ALL_ROWS, :]
    for copy in sent:
        copy.wait()


def presmooth(count, got_a, got_b, raw, tx, ty, tz, dg, w0, w1, w2, operator):
    results = pl.pallas_call(
        presmooth_kernel,
        out_shape=(padded(),) * 4
        + (padded_out(),) * 9
        + (jax.ShapeDtypeStruct((count * ALL_ROWS, LANES), F32),)
        + (payload(),) * 2,
        in_specs=in_vmem(11),
        out_specs=tuple(in_vmem(4) + in_hbm(9) + in_vmem(3)),
        input_output_aliases={3: 0, 4: 1, 5: 2, 6: 3},
        scratch_shapes=[padded()] * 4
        + [
            vmem((PHASES, NCY, 64, LANES)),
            vmem((PAIR * 24, LANES)),
            vmem((TILES * 16, LANES)),
        ]
        + tails()
        + [semaphores(9)],
        compiler_params=params(16),
    )(got_a, got_b, raw, tx, ty, tz, dg, w0, w1, w2, operator)
    return results[4:]


def regrouped(ref, dst, shift, index, load):
    lane = lanes_of(OWN)
    rolled = {}

    def piece(quarter, t):
        offset = 3200 * quarter + NZ * shift - NZ * quarter
        first, turn = (t * LANES + offset) // LANES, offset % LANES

        def source(tile):
            tile = min(max(tile, 0), TILES - 1)
            key = (tile, turn)
            if key not in rolled:
                value = load(ref, tile)
                rolled[key] = lane_roll(value, -turn) if turn else value
            return rolled[key]

        if quarter * GROUP + shift < 0 or quarter * GROUP + shift >= 4 * GROUP:
            return None
        low_lane, high_lane = max(0, quarter * NZ - t * LANES), min(LANES, (quarter + 1) * NZ - t * LANES)
        if turn == 0 or high_lane <= LANES - turn:
            return source(first)
        if low_lane >= LANES - turn:
            return source(first + 1)
        return jnp.where(lane < LANES - turn, source(first), source(first + 1))

    for t in range(LT):
        first = t * LANES // NZ
        last = (t * LANES + LANES - 1) // NZ
        value = piece(first, t)
        if last != first:
            other = piece(last, t)
            value = jnp.zeros((OWN, LANES), F32) if value is None else value
            other = jnp.zeros((OWN, LANES), F32) if other is None else other
            value = jnp.where(lane < last * NZ - t * LANES, value, other)
        elif value is None:
            value = jnp.zeros((OWN, LANES), F32)
        dst[index, t, 0:OWN, :] = value
        dst[index, t, OWN:PAD, :] = jnp.zeros((PAD - OWN, LANES), F32)


def assemble_kernel(
    rhs_in, accum_in, x_in, y_in, z_in, center_in, lower_in, upper_in, inverse, before,
    out, raw, tx_n, ty_n, tz_n, dg_n, w0_n, w1_n, w2_n,
    rhs_v, accum_v, x_v, y_v, z_v, center_v, lower_v, upper_v,
    w, tx, ty, tz, dg, fields, rows_in, found, sems,
):
    wait = stream(
        (rhs_in, accum_in, x_in, y_in, z_in, center_in, lower_in, upper_in),
        (rhs_v, accum_v, x_v, y_v, z_v, center_v, lower_v, upper_v),
        sems,
    )
    weights = (w0_n, w1_n, w2_n)
    lane = lanes_of(OWN)

    def load(t, i, carry):
        z_before, y_before, y_second = carry
        for ref, src in zip(weights, (center_v, lower_v, upper_v)):
            ref[span(t, TOP, OWN), :] = own(src, t)
            ref[span(t, TOP + OWN, 4), :] = jnp.zeros((4, LANES), F32)
        z_pos = (i * LANES + lane) % NZ
        cells = t * LANES + lane
        here = span(t, TOP, OWN)
        x, y, z = own(x_v, t), own(y_v, t), own(z_v, t)
        y_inner = jnp.where(cells < PLANE - NZ, y, 0.0)
        z_inner = jnp.where(z_pos != NZ - 1, z, 0.0)
        z_rolled = lane_roll(z_inner, 1)
        y_rolled = lane_roll(y_inner, NZ - LANES)
        tx_n[span(t, 0, TOP), :] = jnp.zeros((TOP, LANES), F32)
        tx_n[here, :] = x
        ty_n[here, :] = y_inner
        tz_n[here, :] = z_inner
        total = own(accum_v, t) + x + tx_n[span(t, TOP - 1, OWN), :]
        total = total + y + jnp.where(lane < NZ - LANES, y_second, y_before)
        total = total + z + jnp.where(lane == 0, z_before, z_rolled)
        dg_n[here, :] = total
        raw[here, :] = rhs_v[:, at(t)]
        return z_rolled, y_rolled, y_before

    zero = lanes_of(OWN).astype(F32) * 0.0
    over_tiles(load, (zero, zero, zero), wait)

    def plain(ref, tile):
        return ref[tile * PAD + TOP : tile * PAD + TOP + OWN, :]

    for g in range(GROUP):
        regrouped(tx_n, tx, g, g, plain)
        regrouped(ty_n, ty, g, g, plain)
        regrouped(tz_n, tz, g, g, plain)
        regrouped(dg_n, dg, g, g, plain)
    for g in range(GROUP + 1):
        for a, weight in enumerate(weights):
            regrouped(weight, w.at[a], g, g, plain)

    lane8 = lanes_of(8)

    def combo(index, carry):
        half = index // (LT * 3)
        t = (index // 3) % LT
        low = (index % 3) * 8
        t_next = jnp.minimum(t + 1, LT - 1)
        same = pl.ds(pl.multiple_of(low, 8), 8)
        after = pl.ds(low + 1, 8)
        d_sum = [None] * 6
        x_sum = [None] * 9
        z_sum = [None] * 9
        for step in range(BLK):
            g = half * BLK + step
            here = [w[a, g, t, same, :] for a in range(3)]
            x_up = [w[a, g, t, after, :] for a in range(3)]
            y_up = [w[a, g + 1, t, same, :] for a in range(3)]
            z_up = [
                jnp.where(
                    lane8 == LANES - 1,
                    lane_roll(w[a, g, t_next, same, :], -1),
                    lane_roll(here[a], -1),
                )
                for a in range(3)
            ]
            d_t, x_t = dg[g, t, same, :], tx[g, t, same, :]
            y_t, z_t = ty[g, t, same, :], tz[g, t, same, :]
            d_w = [d_t * v for v in here]
            x_w = [x_t * v for v in here]
            y_w = [y_t * v for v in here]
            z_w = [z_t * v for v in here]
            for n, (a, c) in enumerate(PAIRED):
                term = d_w[a] * here[c]
                if step < BLK - 1:
                    cross = y_w[a] * y_up[c]
                    cross = cross + (cross if a == c else y_w[c] * y_up[a])
                    term = term - cross
                d_sum[n] = term if d_sum[n] is None else d_sum[n] + term
            for a in range(3):
                for c in range(3):
                    n = 3 * a + c
                    x_term = x_w[a] * x_up[c]
                    z_term = z_w[a] * z_up[c]
                    x_sum[n] = x_term if x_sum[n] is None else x_sum[n] + x_term
                    z_sum[n] = z_term if z_sum[n] is None else z_sum[n] + z_term
                    if step == BLK - 1:
                        fields[24 + n, half, t, same, :] = y_w[a] * y_up[c]
        for n in range(6):
            fields[n, half, t, same, :] = d_sum[n]
        for n in range(9):
            fields[6 + n, half, t, same, :] = x_sum[n]
            fields[15 + n, half, t, same, :] = z_sum[n]
        return carry

    lax.fori_loop(0, 2 * LT * 3, combo, 0)

    row8 = rows_of(8)

    def fold(index, carry):
        half = index // LT
        t = index % LT
        cols = pl.ds(pl.multiple_of(half * LANES, LANES), LANES)

        def tiles_of(n):
            return [fields[n, half, t, 8 * s : 8 * s + 8, :] for s in range(3)]

        def blocks(v, first):
            return (
                v[0] + jnp.where(row8 < first, v[1], 0.0),
                jnp.where(row8 >= 2, v[1], 0.0) + v[2],
            )

        x_tiles = [tiles_of(6 + n) for n in range(9)]
        x_in = [blocks(v, 1) for v in x_tiles]
        for n, (a, c) in enumerate(PAIRED):
            both = blocks(tiles_of(n), 2)
            for s in range(2):
                value = both[s] - x_in[3 * a + c][s] - x_in[3 * c + a][s]
                rows_in[t, 16 * n + 8 * s : 16 * n + 8 * s + 8, cols] = value
        for n in range(9):
            rows_in[t, 96 + 8 * n : 104 + 8 * n, cols] = jnp.where(row8 == 1, x_tiles[n][1], 0.0)
            for first, base in ((24, 168), (15, 312)):
                both = blocks(tiles_of(first + n), 2)
                for s in range(2):
                    low = base + 16 * n + 8 * s
                    rows_in[t, low : low + 8, cols] = both[s]
        return carry

    lax.fori_loop(0, 2 * LT, fold, 0)

    src = lax.broadcasted_iota(jnp.int32, (2 * LANES, 2 * LANES), 0)
    dst = lax.broadcasted_iota(jnp.int32, (2 * LANES, 2 * LANES), 1)
    total = jnp.zeros((456, 2 * LANES), F32)
    for t in range(LT):
        place = t * LANES + src % LANES
        coarse = place // NZ * 2 * NCZ + src // LANES * NCZ + place % NZ // BLK
        column = coarse + jnp.where(place % BLK == BLK - 1, LANES, 0)
        pick = jnp.where(column == dst, 1.0, 0.0).astype(BF16)
        for piece in halves(rows_in[t]):
            total = total + jnp.dot(piece, pick, preferred_element_type=F32)
    found[0:57, :] = jnp.sum(total.reshape(57, 8, 2 * LANES), axis=1)

    def both(row):
        return found[row : row + 1, 0:LANES] + found[row : row + 1, LANES:]

    def inside(row):
        return found[row : row + 1, 0:LANES]

    def crossing(row):
        return found[row : row + 1, LANES:]

    shares, y_shares, z_shares = {}, {}, {}
    for block in range(2):
        rows = [1 + block + OFFSET[a] for a in range(3)]
        for n, (a, c) in enumerate(PAIRED):
            value = both(2 * n + block)
            value = value - inside(39 + 2 * (3 * a + c) + block) - inside(39 + 2 * (3 * c + a) + block)
            add_share(shares, rows[a], rows[c], value)
        for a in range(3):
            for c in range(3):
                n = 3 * a + c
                pair = (rows[a], rows[c])
                for kept, value in (
                    (y_shares, both(21 + 2 * n + block)),
                    (z_shares, crossing(39 + 2 * n + block)),
                ):
                    kept[pair] = kept[pair] - value if pair in kept else -value
                if block == 0:
                    add_face(shares, 1 + OFFSET[a], 2 + OFFSET[c], both(12 + n))
    out[...] = jnp.zeros_like(out)
    for first, pairs, kept in ((0, SAME, shares), (Y_ROW, ACROSS, y_shares), (Z_ROW, ACROSS, z_shares)):
        for n, pair in enumerate(pairs):
            if pair in kept:
                out[first + n : first + n + 1, :] = kept[pair]
    out[INVERSE_ROW : INVERSE_ROW + 2, :] = inverse[...]


def assemble(rhs, accum, trans_x, trans_y, trans_z, center, lower, upper, inverse, before):
    slab = (LT, PAD, LANES)
    return pl.pallas_call(
        assemble_kernel,
        out_shape=(vmem((ALL_ROWS, LANES)),) + (padded(),) * 8,
        in_specs=in_hbm(8) + in_vmem(1) + [pl.BlockSpec(memory_space=pl.ANY)],
        out_specs=tuple(in_vmem(9)),
        scratch_shapes=[cells(F32)]
        + [cells()] * 7
        + [
            vmem((3, GROUP + 1) + slab),
            vmem((GROUP,) + slab),
            vmem((GROUP,) + slab),
            vmem((GROUP,) + slab),
            vmem((GROUP,) + slab),
            vmem((33, 2, LT, 24, LANES)),
            vmem((LT, 456, 2 * LANES)),
            vmem((57, 2 * LANES)),
            semaphores(8, PAIRS),
        ],
        compiler_params=params(32),
    )(rhs, accum, trans_x, trans_y, trans_z, center, lower, upper, inverse, before)


EDGE = 8


def coarse_solve(count, gathered, same, same_t, y_mat, y_mat_t, z_mat, z_mat_t, inv, rhs, e, e_y, e_z):
    rows = 2 * count
    here = pl.ds(EDGE, rows)
    for ref in (same, y_mat, z_mat, inv, rhs, e, e_y, e_z):
        ref[...] = jnp.zeros_like(ref)

    def share(row):
        return gathered[pl.ds(row, count, ALL_ROWS), :]

    def add(ref, u, value):
        place = pl.ds(EDGE - 1 + u, count, 2)
        ref[place, :] = ref[place, :] + value

    for n, (u, v) in enumerate(SAME):
        add(same.at[v - u], u, share(n))
    for n, (u, v) in enumerate(ACROSS):
        add(y_mat.at[v - u + 2], u, share(Y_ROW + n))
        add(z_mat.at[v - u + 2], u, share(Z_ROW + n))
    for u in range(4):
        add(rhs, u, share(RHS_ROW + u))
    for block in range(2):
        inv[pl.ds(EDGE + block, count, 2), :] = OMEGA_COARSE * share(INVERSE_ROW + block)
    for step in range(1, 4):
        same_t[step - 1] = same[step, pl.ds(EDGE - step, rows), :]
    for step in range(-2, 3):
        y_mat_t[step + 2] = y_mat[step + 2, pl.ds(EDGE - step, rows), :]
        z_mat_t[step + 2] = z_mat[step + 2, pl.ds(EDGE - step, rows), :]
    e[here, :] = inv[here, :] * rhs[here, :]

    def one(index, carry):
        at_step = {step: e[pl.ds(EDGE + step, rows), :] for step in range(-3, 4)}
        e_y[here, :] = lane_roll(at_step[0], -NCZ)
        e_z[here, :] = lane_roll(at_step[0], -1)
        image = same[0, here, :] * at_step[0]
        for step in range(1, 4):
            image = image + same[step, here, :] * at_step[step] + same_t[step - 1] * at_step[-step]
        y_back = z_back = None
        for step in range(-2, 3):
            y_term = y_mat_t[step + 2] * at_step[-step]
            z_term = z_mat_t[step + 2] * at_step[-step]
            y_back = y_term if y_back is None else y_back + y_term
            z_back = z_term if z_back is None else z_back + z_term
        image = image + lane_roll(y_back, NCZ) + lane_roll(z_back, 1)
        for step in range(-2, 3):
            place = pl.ds(EDGE + step, rows)
            image = image + y_mat[step + 2, here, :] * e_y[place, :]
            image = image + z_mat[step + 2, here, :] * e_z[place, :]
        e[here, :] = at_step[0] + inv[here, :] * (rhs[here, :] - image)
        return carry

    lax.fori_loop(0, CSW - 1, one, 0)


def finish_kernel(
    count, gathered_rows, got_a, got_b, smooth_in, tx_in, ty_in, tz_in, k_in, b_in, w0_in, w1_in, w2_in,
    out, update,
    smooth, tx, ty, tz, k, b, w0, w1, w2,
    same, same_t, y_mat, y_mat_t, z_mat, z_mat_t, inv, rhs, e, e_y, e_z, strips, spread, first, second, tail_a, tail_b, sems,
):
    weights = (w0, w1, w2)
    coming = copies(
        (smooth_in, w0_in, w1_in, w2_in, tx_in, ty_in, tz_in, k_in, b_in),
        (smooth, w0, w1, w2, tx, ty, tz, k, b),
        sems,
    )
    coarse_solve(
        count, gathered_rows, same, same_t, y_mat, y_mat_t, z_mat, z_mat_t, inv, rhs, e, e_y, e_z
    )
    base = EDGE + 2 * lax.axis_index("gx")
    update[...] = e[pl.ds(base, 2), :]
    near = {s: e[pl.ds(base + s, 1), :] for s in range(-2, 4)}
    row = rows_of(PAD)
    lane = lanes_of(PAD)
    for a, s in enumerate((0, -1, 1)):
        value = jnp.where(row < TOP + BLK, near[s], near[s + 1])
        value = jnp.where(row < TOP, near[s - 1], value)
        value = jnp.where(row >= TOP + OWN, near[s + 2], value)
        high = value.astype(BF16).astype(F32)
        rest = value - high
        low = rest.astype(BF16).astype(F32)
        rest = rest - low
        for strip in range(NCY):
            turned = lane_roll(high, -strip * NCZ)
            turned = jnp.where(lane < NCZ, turned, lane_roll(low, (1 - strip) * NCZ))
            turned = jnp.where(lane < 2 * NCZ, turned, lane_roll(rest, (2 - strip) * NCZ))
            turned = jnp.where(lane < 3 * NCZ, turned, 0.0)
            strips[a, strip] = turned.astype(BF16)
    src = lax.broadcasted_iota(jnp.int32, (LANES, LANES), 0)
    dst = lax.broadcasted_iota(jnp.int32, (LANES, LANES), 1)
    flat = strips[...].reshape(3 * NCY * PAD, LANES)
    for phase in range(PHASES):
        pick = jnp.where((phase * LANES + dst) % NZ // BLK == src % NCZ, 1.0, 0.0).astype(BF16)
        got = jnp.dot(flat, pick, preferred_element_type=F32)
        spread[phase] = got.reshape(3, NCY, PAD, LANES)

    for copy in coming:
        copy.wait()
    both = received(got_a, got_b, tail_a, tail_b)
    for q in range(WHOLE + 1):
        size = 16 if q < WHOLE else REST
        values = [both(n, q) for n in range(PLANES)]
        for side, rows in ((0, (7, 6, 5)), (1, (28, 29, 30))):
            got = [v[side] for v in values]
            for n, row in enumerate(rows):
                smooth[plane(smooth, row, q, size), :] = got[2 * n] + got[2 * n + 1]
                for a, w in enumerate(weights):
                    w[plane(w, row, q, size), :] = got[6 + 3 * a + n]

    def prolong(t, i, carry):
        n = t // PAIR
        phase = i % PHASES
        here = span(t, 0, PAD)
        total = smooth[here, :]
        for a, w in enumerate(weights):
            if i == PAIR // 2:
                values = jnp.where(
                    lane < LANES // 2, spread[phase, a, 2 * n], spread[phase, a, 2 * n + 1]
                )
            else:
                values = spread[phase, a, 2 * n + (1 if i > PAIR // 2 else 0)]
            total = total + w[here, :] * values
        first[here, :] = total
        return carry

    over_tiles(prolong, 0)
    sweep(first, second, tx, ty, tz, k, b, 6, 24)
    sweep(second, first, tx, ty, tz, k, b, 7, 22)

    def last(t, i, carry):
        total, after = coupled(first, tx, ty, tz, t, TOP, OWN, carry)
        here = span(t, TOP, OWN)
        out[:, at(t)] = b[here, :] + (1.0 - OMEGA_FINE) * carry[0] + k[here, :] * total
        return after

    over_tiles(last, coupled_start(first, TOP, OWN))


def finish(gathered_rows, got_a, got_b, smooth, tx, ty, tz, k, b, w0, w1, w2):
    count = gathered_rows.shape[0] // ALL_ROWS
    rows = 2 * count

    def kernel(*refs):
        finish_kernel(count, *refs)

    return pl.pallas_call(
        kernel,
        out_shape=(
            jax.ShapeDtypeStruct((OWN, PLANE), F32),
            jax.ShapeDtypeStruct((2, LANES), F32),
        ),
        in_specs=in_vmem(3) + in_hbm(9),
        out_specs=tuple(in_vmem(2)),
        scratch_shapes=[padded()] * 9
        + [
            vmem((4, rows + 2 * EDGE, LANES)),
            vmem((3, rows, LANES)),
            vmem((5, rows + 2 * EDGE, LANES)),
            vmem((5, rows, LANES)),
            vmem((5, rows + 2 * EDGE, LANES)),
            vmem((5, rows, LANES)),
        ]
        + [vmem((rows + 2 * EDGE, LANES))] * 5
        + [
            vmem((3, NCY, PAD, LANES), BF16),
            vmem((PHASES, 3, NCY, PAD, LANES)),
            vmem((TILES * PAD, LANES)),
            vmem((TILES * PAD, LANES)),
        ]
        + tails()
        + [semaphores(9)],
        compiler_params=params(58),
    )(gathered_rows, got_a, got_b, smooth, tx, ty, tz, k, b, w0, w1, w2)


def swapped(pay_a, pay_b):
    count = lax.axis_size("gx")
    got_a = lax.ppermute(pay_a, "gx", [(i, i ^ 1) for i in range(count)])
    inner = [(i, i + 1 if i % 2 else i - 1) for i in range(1, count - 1)]
    return got_a, lax.ppermute(pay_b, "gx", inner)


def spread_out(rows):
    count = lax.axis_size("gx")
    each = rows.shape[0] // count
    got = lax.all_to_all(rows.reshape(count, each, LANES), "gx", 0, 0)
    return got.reshape(count * each, LANES)


def per_device(
    rhs, accumulation, trans_x, trans_y, trans_z, basis_center, basis_side, coarse_inverse
):
    count = lax.axis_size("gx")
    pay_a, pay_b = prepare(
        rhs, accumulation, trans_x, trans_y, trans_z, basis_center, basis_side[:, 0]
    )
    got_a, got_b = swapped(pay_a, pay_b)
    operator, *own_fields = assemble(
        rhs, accumulation, trans_x, trans_y, trans_z, basis_center, basis_side[0], basis_side[1],
        coarse_inverse, pay_b,
    )
    *kept, part, pay_a, pay_b = presmooth(count, got_a, got_b, *own_fields, operator)
    got_a, got_b = swapped(pay_a, pay_b)
    gathered = spread_out(part)
    tx, ty, tz, k, b, smooth, w0, w1, w2 = kept
    return finish(gathered, got_a, got_b, smooth, tx, ty, tz, k, b, w0, w1, w2)


def solution(mesh):
    both = ("grp", "gx")
    cells = P(both, None)
    return jax.shard_map(
        per_device,
        mesh=mesh,
        in_specs=(cells,) * 6 + (P(None, both, None), cells),
        out_specs=(cells, cells),
        check_vma=False,
    )
```

```python
import jax
import jax.numpy as jnp
from jax import lax
from jax.experimental import pallas as pl
from jax.experimental.pallas import tpu as pltpu
from jax.sharding import PartitionSpec as P

BLK = 10
NCY = 8
NCZ = 16
CSW = 6
NZ = 160
PLANE = 12800
COARSE = NCY * NCZ
OMEGA_FINE = 0.7
OMEGA_COARSE = 0.6

LANES = 128
TILES = PLANE // LANES
PHASES = 5
PAIR = 25
PAIRS = TILES // PAIR
OWN = 20
TOP = 3
PAD = OWN + 2 * TOP
HEAD = (TOP, TOP + 1, TOP + 2)
LAST = (TOP + OWN - 1, TOP + OWN - 2, TOP + OWN - 3)
BEFORE = (TOP - 1, TOP - 2, TOP - 3)
BEYOND = (TOP + OWN, TOP + OWN + 1, TOP + OWN + 2)
SPREAD = 32
GROUP = 20
QUARTERS = 4
LT = QUARTERS * NZ // LANES
PAIRED = ((0, 0), (0, 1), (0, 2), (1, 1), (1, 2), (2, 2))
FIRST = 17
SECOND = 10
WHOLE = TILES // 16
REST = TILES % 16
OFFSET = (0, -1, 1)
SAME = ((0, 0), (0, 1), (0, 2), (0, 3), (1, 1), (1, 2), (1, 3), (2, 2), (2, 3), (3, 3), (1, 4), (2, 4), (3, 4))
ACROSS = tuple((u, v) for u in range(4) for v in range(4) if abs(u - v) <= 2)
Y_ROW = len(SAME)
Z_ROW = Y_ROW + len(ACROSS)
INVERSE_ROW = Z_ROW + len(ACROSS)
RHS_ROW = INVERSE_ROW + 2
ALL_ROWS = 48
F32 = jnp.float32
BF16 = jnp.bfloat16


def params(mib):
    return pltpu.CompilerParams(vmem_limit_bytes=mib << 20)


def lasting(microseconds):
    return pl.CostEstimate(
        flops=0, transcendentals=0, bytes_accessed=int(3.5e6 * microseconds)
    )


def vmem(shape, dtype=F32):
    return pltpu.VMEM(shape, dtype)


def in_vmem(count):
    return [pl.BlockSpec(memory_space=pltpu.VMEM)] * count


def in_hbm(count):
    return [pl.BlockSpec(memory_space=pltpu.HBM)] * count


def padded():
    return vmem((TILES * PAD + 8, LANES))


def padded_out():
    return pltpu.HBM((TILES * PAD + 8, LANES), F32)


def cells(dtype=BF16):
    return vmem((OWN, PLANE), dtype)


def semaphores(*shape):
    return pltpu.SemaphoreType.DMA(shape)


def stream(sources, buffers, sems):
    width = PLANE // PAIRS

    def copy(field, n):
        lanes = pl.ds(pl.multiple_of(n * width, width), width)
        return pltpu.make_async_copy(
            sources[field].at[:, lanes], buffers[field].at[:, lanes], sems.at[field, n]
        )

    for n in range(PAIRS):
        for field in range(len(sources)):
            copy(field, n).start()

    def wait(n):
        for field in range(len(sources)):
            copy(field, n).wait()

    return wait


def copies(sources, targets, sems):
    made = [
        pltpu.make_async_copy(src, dst, sems.at[n])
        for n, (src, dst) in enumerate(zip(sources, targets))
    ]
    for copy in made:
        copy.start()
    return made


def lane_roll(value, steps):
    return pltpu.roll(value, steps % LANES, 1)


def lanes_of(rows):
    return lax.broadcasted_iota(jnp.int32, (rows, LANES), 1)


def rows_of(rows):
    return lax.broadcasted_iota(jnp.int32, (rows, LANES), 0)


def at(t):
    return pl.ds(pl.multiple_of(t * LANES, LANES), LANES)


def span(t, low, count):
    return pl.ds(t * PAD + low, count)


def own(ref, t):
    return ref[:, at(t)].astype(F32)


def over_tiles(body, carry, before=None, unroll=1):
    def step(n, carry):
        if before is not None:
            before(n)
        for i in range(PAIR):
            carry = body(n * PAIR + i, i, carry)
        return carry

    return lax.fori_loop(0, PAIRS, step, carry, unroll=unroll)


def halves(value):
    high = value.astype(BF16)
    low = (value - high.astype(F32)).astype(BF16)
    return high, low


def remainder(value):
    return value - value.astype(BF16).astype(F32)


def parity():
    return lax.rem(lax.axis_index("gx"), 2)


def coupled(src, tx, ty, tz, t, low, count, carry):
    center, following, y_next, z_flux, y_flux, y_flux_before = carry
    lane = lanes_of(count)
    here = span(t, low, count)
    second = src[span(jnp.minimum(t + 2, TILES - 1), low, count), :]
    z_up = jnp.where(lane == LANES - 1, lane_roll(following, -1), lane_roll(center, -1))
    y_second = lane_roll(second, -(NZ - LANES))
    y_up = jnp.where(lane >= 2 * LANES - NZ, y_second, y_next)
    tz_t = tz[here, :]
    ty_t = ty[here, :]
    z_flux_new = lane_roll(tz_t * center, 1)
    z_down = jnp.where(lane == 0, z_flux, z_flux_new)
    y_down = jnp.where(lane < NZ - LANES, y_flux_before, y_flux)
    y_flux_new = lane_roll(ty_t * center, NZ - LANES)
    total = tz_t * z_up + z_down
    total = total + (ty_t * y_up + y_down)
    total = total + tx[here, :] * src[span(t, low + 1, count), :]
    total = total + tx[span(t, low - 1, count), :] * src[span(t, low - 1, count), :]
    return total, (following, second, y_second, z_flux_new, y_flux_new, y_flux)


def coupled_start(src, low, count):
    center = src[span(0, low, count), :]
    following = src[span(1, low, count), :]
    zero = center * 0.0
    return center, following, lane_roll(following, -(NZ - LANES)), zero, zero, zero


def sweep(src, dst, tx, ty, tz, k, b, low, count):
    def body(t, i, carry):
        total, after = coupled(src, tx, ty, tz, t, low, count, carry)
        here = span(t, low, count)
        dst[here, :] = b[here, :] + (1.0 - OMEGA_FINE) * carry[0] + k[here, :] * total
        return after

    over_tiles(body, coupled_start(src, low, count), unroll=4)


def plane(ref, row, q, size, stride=PAD):
    return pl.ds(16 * q * stride + row, size, stride)


def read_plane(ref, row, stride=PAD):
    return lambda q, size: ref[plane(ref, row, q, size, stride), :]


def send_both(pay_a, pay_b, tail_a, tail_b, right, left):
    even = parity() == 0
    count = len(right)
    for n in range(count):
        for q in range(WHOLE + 1):
            size = 16 if q < WHOLE else REST
            r, l = right[n](q, size), left[n](q, size)
            a, b = jnp.where(even, r, l), jnp.where(even, l, r)
            if q < WHOLE:
                rows = slice((n * WHOLE + q) * 16, (n * WHOLE + q) * 16 + 16)
                pay_a[rows, :] = a.astype(BF16)
                pay_b[rows, :] = b.astype(BF16)
            else:
                rows = slice(n * REST, n * REST + REST)
                tail_a[rows, :] = a
                tail_b[rows, :] = b
    pay_a[count * WHOLE * 16 :, :] = tail_a[...].astype(BF16)
    pay_b[count * WHOLE * 16 :, :] = tail_b[...].astype(BF16)


def received(count, got_a, got_b, tail_a, tail_b):
    even = parity() == 0
    tail_a[...] = got_a[count * WHOLE * 16 :, :].astype(F32)
    tail_b[...] = got_b[count * WHOLE * 16 :, :].astype(F32)

    def both(n, q):
        if q < WHOLE:
            rows = slice((n * WHOLE + q) * 16, (n * WHOLE + q) * 16 + 16)
            a, b = got_a[rows, :].astype(F32), got_b[rows, :].astype(F32)
        else:
            rows = slice(n * REST, n * REST + REST)
            a, b = tail_a[rows, :], tail_b[rows, :]
        return jnp.where(even, b, a), jnp.where(even, a, b)

    return both


def payload_rows(count):
    return -(-count * TILES // 16) * 16


def payload(count):
    return jax.ShapeDtypeStruct((payload_rows(count), LANES), BF16)


def tails(count):
    return [vmem((payload_rows(count) - count * WHOLE * 16, LANES))] * 2


def low_part(f):
    return lambda q, size: remainder(f(q, size))


def prepare_kernel(
    rhs_in, accum_in, x_in, y_in, z_in, center_in, side_in,
    raw, tx_n, ty_n, tz_n, dg_n, w0_n, w1_n, w2_n, pay_a, pay_b,
    rhs_v, accum_v, x_v, y_v, z_v, center_v, lower_v, upper_v, tail_a, tail_b, sems,
):
    wait = stream(
        (rhs_in, accum_in, x_in, y_in, z_in, center_in, side_in.at[0], side_in.at[1]),
        (rhs_v, accum_v, x_v, y_v, z_v, center_v, lower_v, upper_v),
        sems,
    )
    weights = (w0_n, w1_n, w2_n)
    lane = lanes_of(OWN)

    def load(t, i, carry):
        z_before, y_before, y_second = carry
        for ref, src in zip(weights, (center_v, lower_v, upper_v)):
            ref[span(t, TOP, OWN), :] = own(src, t)
        z_pos = (i * LANES + lane) % NZ
        cells = t * LANES + lane
        here = span(t, TOP, OWN)
        x, y, z = own(x_v, t), own(y_v, t), own(z_v, t)
        y_inner = jnp.where(cells < PLANE - NZ, y, 0.0)
        z_inner = jnp.where(z_pos != NZ - 1, z, 0.0)
        z_rolled = lane_roll(z_inner, 1)
        y_rolled = lane_roll(y_inner, NZ - LANES)
        tx_n[span(t, TOP - 1, 1), :] = jnp.zeros((1, LANES), F32)
        tx_n[here, :] = x
        ty_n[here, :] = y_inner
        tz_n[here, :] = z_inner
        total = own(accum_v, t) + x + tx_n[span(t, TOP - 1, OWN), :]
        total = total + y + jnp.where(lane < NZ - LANES, y_second, y_before)
        total = total + z + jnp.where(lane == 0, z_before, z_rolled)
        dg_n[here, :] = total
        raw[here, :] = rhs_v[:, at(t)]
        return z_rolled, y_rolled, y_before

    zero = lanes_of(OWN).astype(F32) * 0.0
    over_tiles(load, (zero, zero, zero), wait)

    def first_sweep(row):
        r, d = read_plane(raw, row), read_plane(dg_n, row)
        return lambda q, size: OMEGA_FINE * r(q, size) / d(q, size)

    def planes(rows, x_rows):
        near, second, far = rows
        r, d = read_plane(raw, near), read_plane(dg_n, near)
        found = [r, low_part(r), read_plane(raw, second)]
        found += [d, low_part(d), read_plane(dg_n, second)]
        found += [read_plane(ref, row) for ref in (ty_n, tz_n) for row in (near, second)]
        found += [first_sweep(far)]
        found += [read_plane(tx_n, row) for row in x_rows]
        found += [read_plane(w, near) for w in weights]
        return found

    right, left = LAST, HEAD
    send_both(pay_a, pay_b, tail_a, tail_b, planes(right, right), planes(left, left))


def prepare(*fields):
    return pl.pallas_call(
        prepare_kernel,
        out_shape=(padded(),) * 8 + (payload(FIRST),) * 2,
        in_specs=in_hbm(7),
        out_specs=tuple(in_vmem(10)),
        scratch_shapes=[cells(F32)] + [cells()] * 7 + tails(FIRST) + [semaphores(8, PAIRS)],
        compiler_params=params(46),
        cost_estimate=lasting(6),
    )(*fields)


def add_share(shares, u, v, value):
    pair = (min(u, v), max(u, v))
    shares[pair] = shares[pair] + value if pair in shares else value


def add_face(shares, u, v, value):
    add_share(shares, u, v, -2.0 * value if u == v else -value)


def presmooth_kernel(
    got_a, got_b, raw, tx_in, ty_in, tz_in, dg_in, w0_in, w1_in, w2_in, after,
    tx, ty, tz, dg, w0, w1, w2,
    k, b, smooth, edges, pay_a, pay_b,
    work, tail_a, tail_b, second_a, second_b,
):
    weights = (w0, w1, w2)
    both = received(FIRST, got_a, got_b, tail_a, tail_b)
    for q in range(WHOLE + 1):
        size = 16 if q < WHOLE else REST

        def put(ref, row, value):
            ref[plane(ref, row, q, size), :] = value

        def get(ref, row):
            return ref[plane(ref, row, q, size), :]

        values = [both(n, q) for n in range(FIRST)]
        left, right = [v[0] for v in values], [v[1] for v in values]
        for got, rows in ((left, BEFORE), (right, BEYOND)):
            put(b, rows[0], got[0] + got[1])
            put(b, rows[1], got[2])
            put(dg, rows[1], got[5])
            put(ty, rows[0], got[6])
            put(ty, rows[1], got[7])
            put(tz, rows[0], got[8])
            put(tz, rows[1], got[9])
            put(b, rows[2], got[10])
            put(tx, rows[0], got[11])
            put(tx, rows[1], got[12])
            for a, w in enumerate(weights):
                put(w, rows[0], got[14 + a])
        put(tx, BEFORE[2], left[13])
        tx_before = left[11]
        tx_last = get(tx, TOP + OWN - 1)
        beyond = right[3] + right[4]
        put(dg, BEFORE[0], left[3] + left[4])
        put(dg, BEYOND[0], jnp.where(beyond > 0.0, beyond + tx_last, 0.0))
        put(dg, TOP, get(dg, TOP) + tx_before)
        first = [get(w, TOP) for w in weights]
        last = [get(w, TOP + OWN - 1) for w in weights]
        from_next = [right[14 + a] for a in range(3)]
        products = [tx_last * last[a] * from_next[c] for a in range(3) for c in range(3)]
        products += [tx_before * first[a] * first[c] for a, c in PAIRED]
        for n, value in enumerate(products):
            edges[plane(edges, n, q, size, 16), :] = value
        edges[plane(edges, 15, q, size, 16), :] = tx_last * 0.0

    def scale(t, i, carry):
        here = span(t, TOP - 2, OWN + 4)
        diag = dg[here, :]
        value = jnp.where(diag > 0.0, OMEGA_FINE / diag, 0.0)
        k[here, :] = value
        b[span(t, TOP, OWN), :] = raw[span(t, TOP, OWN), :]
        b[here, :] = value * b[here, :]
        return carry

    over_tiles(scale, 0)
    sweep(b, work, tx, ty, tz, k, b, TOP - 2, OWN + 4)
    sweep(work, smooth, tx, ty, tz, k, b, TOP - 1, OWN + 2)

    def planes(rows):
        near = read_plane(smooth, rows[0])
        found = [near, low_part(near), read_plane(smooth, rows[1]), read_plane(smooth, rows[2])]
        return found + [read_plane(w, row) for w in weights for row in rows[1:]]

    send_both(pay_a, pay_b, second_a, second_b, planes(LAST), planes(HEAD))


def presmooth(got_a, got_b, raw, tx, ty, tz, dg, w0, w1, w2, operator):
    return pl.pallas_call(
        presmooth_kernel,
        out_shape=(padded(),) * 10 + (vmem((TILES * 16, LANES)),) + (payload(SECOND),) * 2,
        in_specs=in_vmem(11),
        out_specs=tuple(in_vmem(13)),
        input_output_aliases={n + 3: n for n in range(7)},
        scratch_shapes=[padded()] + tails(FIRST) + tails(SECOND),
        compiler_params=params(8),
        cost_estimate=lasting(6),
    )(got_a, got_b, raw, tx, ty, tz, dg, w0, w1, w2, operator)


def restrict_kernel(
    smooth, raw, tx, ty, tz, dg, w0, w1, w2, edges, operator, part, sums, rest
):
    weights = (w0, w1, w2)
    sums[...] = jnp.zeros_like(sums)
    lane = lanes_of(64)
    row8 = rows_of(8)
    for n in range(PAIR):
        rest[n * 24 + 16 : n * 24 + 24, :] = jnp.zeros((8, LANES), F32)

    def residual(t, i, carry):
        total, following = coupled(smooth, tx, ty, tz, t, TOP, OWN, carry)
        rest[i * 24 : i * 24 + OWN, :] = (
            raw[span(t, TOP, OWN), :] - dg[span(t, TOP, OWN), :] * carry[0] + total
        )
        left_over = rest[i * 24 : i * 24 + 24, :]
        folded = []
        for w in weights:
            f = w[span(t, TOP, 24), :] * left_over
            mixed = jnp.where(row8 < BLK - 8, f[8:16], 0.0)
            folded += [f[0:8] + mixed, jnp.where(row8 < 4, f[16:24], 0.0) + (f[8:16] - mixed)]
        folded = jnp.concatenate(folded + [edges[pl.ds(t * 16, 16), :]], axis=0)
        n = t // PAIR
        phase = i % PHASES
        if i != PAIR // 2:
            sums[phase, 2 * n + (1 if i > PAIR // 2 else 0)] += folded
        else:
            sums[phase, 2 * n] += jnp.where(lane < LANES // 2, folded, 0.0)
            sums[phase, 2 * n + 1] += jnp.where(lane < LANES // 2, 0.0, folded)
        return following

    over_tiles(residual, coupled_start(smooth, TOP, OWN))

    src = lax.broadcasted_iota(jnp.int32, (LANES, LANES), 0)
    dst = lax.broadcasted_iota(jnp.int32, (LANES, LANES), 1)
    found = jnp.zeros((NCY * 64, LANES), F32)
    for phase in range(PHASES):
        pick = jnp.where((phase * LANES + src) % NZ // BLK == dst, 1.0, 0.0).astype(BF16)
        for piece in halves(sums[phase].reshape(NCY * 64, LANES)):
            found = found + jnp.dot(piece, pick, preferred_element_type=F32)
    placed = found[0:64]
    for strip in range(1, NCY):
        placed = placed + lane_roll(found[strip * 64 : strip * 64 + 64], strip * NCZ)
    shares = {}
    for n, (a, c) in enumerate(PAIRED):
        add_share(shares, 1 + OFFSET[a], 1 + OFFSET[c], placed[57 + n : 58 + n])
    for a in range(3):
        for c in range(3):
            add_face(shares, 2 + OFFSET[a], 3 + OFFSET[c], placed[48 + 3 * a + c : 49 + 3 * a + c])
    part[0:ALL_ROWS, :] = operator[...]
    for n, pair in enumerate(SAME):
        if pair in shares:
            part[n : n + 1, :] += shares[pair]
    for a in range(3):
        for block in range(2):
            row = RHS_ROW + 1 + block + OFFSET[a]
            low = (2 * a + block) * 8
            part[row : row + 1, :] += jnp.sum(placed[low : low + 8], axis=0, keepdims=True)


def restrict(smooth, raw, tx, ty, tz, dg, w0, w1, w2, edges, operator):
    return pl.pallas_call(
        restrict_kernel,
        out_shape=vmem((ALL_ROWS, LANES)),
        in_specs=in_vmem(11),
        out_specs=in_vmem(1)[0],
        scratch_shapes=[vmem((PHASES, NCY, 64, LANES)), vmem((PAIR * 24, LANES))],
        compiler_params=params(6),
        cost_estimate=lasting(4),
    )(smooth, raw, tx, ty, tz, dg, w0, w1, w2, edges, operator)


def regrouped(ref, dst, shift, index, load):
    lane = lanes_of(OWN)
    rolled = {}

    def piece(quarter, t):
        offset = 3200 * quarter + NZ * shift - NZ * quarter
        first, turn = (t * LANES + offset) // LANES, offset % LANES

        def source(tile):
            tile = min(max(tile, 0), TILES - 1)
            key = (tile, turn)
            if key not in rolled:
                value = load(ref, tile)
                rolled[key] = lane_roll(value, -turn) if turn else value
            return rolled[key]

        if quarter * GROUP + shift < 0 or quarter * GROUP + shift >= 4 * GROUP:
            return None
        low_lane, high_lane = max(0, quarter * NZ - t * LANES), min(LANES, (quarter + 1) * NZ - t * LANES)
        if turn == 0 or high_lane <= LANES - turn:
            return source(first)
        if low_lane >= LANES - turn:
            return source(first + 1)
        return jnp.where(lane < LANES - turn, source(first), source(first + 1))

    for t in range(LT):
        first = t * LANES // NZ
        last = (t * LANES + LANES - 1) // NZ
        value = piece(first, t)
        if last != first:
            other = piece(last, t)
            value = jnp.zeros((OWN, LANES), F32) if value is None else value
            other = jnp.zeros((OWN, LANES), F32) if other is None else other
            value = jnp.where(lane < last * NZ - t * LANES, value, other)
        elif value is None:
            value = jnp.zeros((OWN, LANES), F32)
        dst[index, t, 0:OWN, :] = value
        dst[index, t, OWN:SPREAD, :] = jnp.zeros((SPREAD - OWN, LANES), F32)


def assemble_kernel(
    tx_n, ty_n, tz_n, dg_n, w0_n, w1_n, w2_n, inverse, out,
    w, tx, ty, tz, dg, fields, rows_in, found,
):
    weights = (w0_n, w1_n, w2_n)

    def plain(ref, tile):
        return ref[tile * PAD + TOP : tile * PAD + TOP + OWN, :]

    for g in range(GROUP):
        regrouped(tx_n, tx, g, g, plain)
        regrouped(ty_n, ty, g, g, plain)
        regrouped(tz_n, tz, g, g, plain)
        regrouped(dg_n, dg, g, g, plain)
    for g in range(GROUP + 1):
        for a, weight in enumerate(weights):
            regrouped(weight, w.at[a], g, g, plain)

    lane8 = lanes_of(8)

    def combo(index, carry):
        half = index // (LT * 3)
        t = (index // 3) % LT
        low = (index % 3) * 8
        t_next = jnp.minimum(t + 1, LT - 1)
        same = pl.ds(pl.multiple_of(low, 8), 8)
        after = pl.ds(low + 1, 8)
        d_sum = [None] * 6
        x_sum = [None] * 9
        z_sum = [None] * 9
        for step in range(BLK):
            g = half * BLK + step
            here = [w[a, g, t, same, :] for a in range(3)]
            x_up = [w[a, g, t, after, :] for a in range(3)]
            y_up = [w[a, g + 1, t, same, :] for a in range(3)]
            z_up = [
                jnp.where(
                    lane8 == LANES - 1,
                    lane_roll(w[a, g, t_next, same, :], -1),
                    lane_roll(here[a], -1),
                )
                for a in range(3)
            ]
            d_t, x_t = dg[g, t, same, :], tx[g, t, same, :]
            y_t, z_t = ty[g, t, same, :], tz[g, t, same, :]
            d_w = [d_t * v for v in here]
            x_w = [x_t * v for v in here]
            y_w = [y_t * v for v in here]
            z_w = [z_t * v for v in here]
            for n, (a, c) in enumerate(PAIRED):
                term = d_w[a] * here[c]
                if step < BLK - 1:
                    cross = y_w[a] * y_up[c]
                    cross = cross + (cross if a == c else y_w[c] * y_up[a])
                    term = term - cross
                d_sum[n] = term if d_sum[n] is None else d_sum[n] + term
            for a in range(3):
                for c in range(3):
                    n = 3 * a + c
                    x_term = x_w[a] * x_up[c]
                    z_term = z_w[a] * z_up[c]
                    x_sum[n] = x_term if x_sum[n] is None else x_sum[n] + x_term
                    z_sum[n] = z_term if z_sum[n] is None else z_sum[n] + z_term
                    if step == BLK - 1:
                        fields[24 + n, half, t, same, :] = y_w[a] * y_up[c]
        for n in range(6):
            fields[n, half, t, same, :] = d_sum[n]
        for n in range(9):
            fields[6 + n, half, t, same, :] = x_sum[n]
            fields[15 + n, half, t, same, :] = z_sum[n]
        return carry

    lax.fori_loop(0, 2 * LT * 3, combo, 0)

    row8 = rows_of(8)

    def fold(index, carry):
        half = index // LT
        t = index % LT
        cols = pl.ds(pl.multiple_of(half * LANES, LANES), LANES)

        def tiles_of(n):
            return [fields[n, half, t, 8 * s : 8 * s + 8, :] for s in range(3)]

        def blocks(v, first):
            return (
                v[0] + jnp.where(row8 < first, v[1], 0.0),
                jnp.where(row8 >= 2, v[1], 0.0) + v[2],
            )

        x_tiles = [tiles_of(6 + n) for n in range(9)]
        x_in = [blocks(v, 1) for v in x_tiles]
        for n, (a, c) in enumerate(PAIRED):
            both = blocks(tiles_of(n), 2)
            for s in range(2):
                value = both[s] - x_in[3 * a + c][s] - x_in[3 * c + a][s]
                rows_in[t, 16 * n + 8 * s : 16 * n + 8 * s + 8, cols] = value
        for n in range(9):
            rows_in[t, 96 + 8 * n : 104 + 8 * n, cols] = jnp.where(row8 == 1, x_tiles[n][1], 0.0)
            for first, base in ((24, 168), (15, 312)):
                both = blocks(tiles_of(first + n), 2)
                for s in range(2):
                    low = base + 16 * n + 8 * s
                    rows_in[t, low : low + 8, cols] = both[s]
        return carry

    lax.fori_loop(0, 2 * LT, fold, 0)

    src = lax.broadcasted_iota(jnp.int32, (2 * LANES, 2 * LANES), 0)
    dst = lax.broadcasted_iota(jnp.int32, (2 * LANES, 2 * LANES), 1)
    total = jnp.zeros((456, 2 * LANES), F32)
    for t in range(LT):
        place = t * LANES + src % LANES
        coarse = place // NZ * 2 * NCZ + src // LANES * NCZ + place % NZ // BLK
        column = coarse + jnp.where(place % BLK == BLK - 1, LANES, 0)
        pick = jnp.where(column == dst, 1.0, 0.0).astype(BF16)
        for piece in halves(rows_in[t]):
            total = total + jnp.dot(piece, pick, preferred_element_type=F32)
    found[0:57, :] = jnp.sum(total.reshape(57, 8, 2 * LANES), axis=1)

    def both(row):
        return found[row : row + 1, 0:LANES] + found[row : row + 1, LANES:]

    def inside(row):
        return found[row : row + 1, 0:LANES]

    def crossing(row):
        return found[row : row + 1, LANES:]

    shares, y_shares, z_shares = {}, {}, {}
    for block in range(2):
        rows = [1 + block + OFFSET[a] for a in range(3)]
        for n, (a, c) in enumerate(PAIRED):
            value = both(2 * n + block)
            value = value - inside(39 + 2 * (3 * a + c) + block) - inside(39 + 2 * (3 * c + a) + block)
            add_share(shares, rows[a], rows[c], value)
        for a in range(3):
            for c in range(3):
                n = 3 * a + c
                pair = (rows[a], rows[c])
                for kept, value in (
                    (y_shares, both(21 + 2 * n + block)),
                    (z_shares, crossing(39 + 2 * n + block)),
                ):
                    kept[pair] = kept[pair] - value if pair in kept else -value
                if block == 0:
                    add_face(shares, 1 + OFFSET[a], 2 + OFFSET[c], both(12 + n))
    out[...] = jnp.zeros_like(out)
    for first, pairs, kept in ((0, SAME, shares), (Y_ROW, ACROSS, y_shares), (Z_ROW, ACROSS, z_shares)):
        for n, pair in enumerate(pairs):
            if pair in kept:
                out[first + n : first + n + 1, :] = kept[pair]
    out[INVERSE_ROW : INVERSE_ROW + 2, :] = inverse[...]


def assemble(tx, ty, tz, dg, w0, w1, w2, inverse):
    slab = (LT, SPREAD, LANES)
    return pl.pallas_call(
        assemble_kernel,
        out_shape=vmem((ALL_ROWS, LANES)),
        in_specs=in_vmem(8),
        out_specs=in_vmem(1)[0],
        scratch_shapes=[
            vmem((3, GROUP + 1) + slab),
            vmem((GROUP,) + slab),
            vmem((GROUP,) + slab),
            vmem((GROUP,) + slab),
            vmem((GROUP,) + slab),
            vmem((33, 2, LT, 24, LANES)),
            vmem((LT, 456, 2 * LANES)),
            vmem((57, 2 * LANES)),
        ],
        compiler_params=params(24),
        cost_estimate=lasting(10),
    )(tx, ty, tz, dg, w0, w1, w2, inverse)


EDGE = 8


def coarse_solve(count, halves_in, gathered, same, same_t, y_mat, y_mat_t, z_mat, z_mat_t, inv, rhs, e, e_y, e_z):
    rows = 2 * count
    here = pl.ds(EDGE, rows)
    for ref in (same, y_mat, z_mat, inv, rhs, e, e_y, e_z):
        ref[...] = jnp.zeros_like(ref)
    index = lax.axis_index("gx")
    for n, distance in enumerate(arrival(count)):
        ref, n = halves_in[n // (count // 2)], n % (count // 2)
        place = pl.multiple_of(lax.bitwise_xor(index, distance) * ALL_ROWS, ALL_ROWS)
        gathered[pl.ds(place, ALL_ROWS), :] = ref[n * ALL_ROWS : n * ALL_ROWS + ALL_ROWS, :]

    def share(row):
        return gathered[pl.ds(row, count, ALL_ROWS), :]

    def add(ref, u, value):
        place = pl.ds(EDGE - 1 + u, count, 2)
        ref[place, :] = ref[place, :] + value

    for n, (u, v) in enumerate(SAME):
        add(same.at[v - u], u, share(n))
    for n, (u, v) in enumerate(ACROSS):
        add(y_mat.at[v - u + 2], u, share(Y_ROW + n))
        add(z_mat.at[v - u + 2], u, share(Z_ROW + n))
    for u in range(4):
        add(rhs, u, share(RHS_ROW + u))
    for block in range(2):
        inv[pl.ds(EDGE + block, count, 2), :] = OMEGA_COARSE * share(INVERSE_ROW + block)
    for step in range(1, 4):
        same_t[step - 1] = same[step, pl.ds(EDGE - step, rows), :]
    for step in range(-2, 3):
        y_mat_t[step + 2] = y_mat[step + 2, pl.ds(EDGE - step, rows), :]
        z_mat_t[step + 2] = z_mat[step + 2, pl.ds(EDGE - step, rows), :]
    e[here, :] = inv[here, :] * rhs[here, :]

    def one(index, carry):
        at_step = {step: e[pl.ds(EDGE + step, rows), :] for step in range(-3, 4)}
        e_y[here, :] = lane_roll(at_step[0], -NCZ)
        e_z[here, :] = lane_roll(at_step[0], -1)
        image = same[0, here, :] * at_step[0]
        for step in range(1, 4):
            image = image + same[step, here, :] * at_step[step] + same_t[step - 1] * at_step[-step]
        y_back = z_back = None
        for step in range(-2, 3):
            y_term = y_mat_t[step + 2] * at_step[-step]
            z_term = z_mat_t[step + 2] * at_step[-step]
            y_back = y_term if y_back is None else y_back + y_term
            z_back = z_term if z_back is None else z_back + z_term
        image = image + lane_roll(y_back, NCZ) + lane_roll(z_back, 1)
        for step in range(-2, 3):
            place = pl.ds(EDGE + step, rows)
            image = image + y_mat[step + 2, here, :] * e_y[place, :]
            image = image + z_mat[step + 2, here, :] * e_z[place, :]
        e[here, :] = at_step[0] + inv[here, :] * (rhs[here, :] - image)
        return carry

    lax.fori_loop(0, CSW - 1, one, 0)


def finish_kernel(
    count, near_rows, far_rows, got_a, got_b, smooth_in, w0_in, w1_in, w2_in, tx, ty, tz, k, b,
    out, update, smooth, w0, w1, w2,
    gathered, same, same_t, y_mat, y_mat_t, z_mat, z_mat_t, inv, rhs, e, e_y, e_z, strips, spread, first, second, tail_a, tail_b,
):
    weights = (w0, w1, w2)
    coarse_solve(
        count, (near_rows, far_rows), gathered, same, same_t, y_mat, y_mat_t, z_mat, z_mat_t, inv, rhs, e, e_y, e_z
    )
    base = EDGE + 2 * lax.axis_index("gx")
    update[...] = e[pl.ds(base, 2), :]
    near = {s: e[pl.ds(base + s, 1), :] for s in range(-2, 4)}
    row = rows_of(SPREAD)
    lane = lanes_of(SPREAD)
    for a, s in enumerate((0, -1, 1)):
        value = jnp.where(row < TOP + BLK, near[s], near[s + 1])
        value = jnp.where(row < TOP, near[s - 1], value)
        value = jnp.where(row >= TOP + OWN, near[s + 2], value)
        high = value.astype(BF16).astype(F32)
        rest = value - high
        low = rest.astype(BF16).astype(F32)
        rest = rest - low
        for strip in range(NCY):
            turned = lane_roll(high, -strip * NCZ)
            turned = jnp.where(lane < NCZ, turned, lane_roll(low, (1 - strip) * NCZ))
            turned = jnp.where(lane < 2 * NCZ, turned, lane_roll(rest, (2 - strip) * NCZ))
            turned = jnp.where(lane < 3 * NCZ, turned, 0.0)
            strips[a, strip] = turned.astype(BF16)
    src = lax.broadcasted_iota(jnp.int32, (LANES, LANES), 0)
    dst = lax.broadcasted_iota(jnp.int32, (LANES, LANES), 1)
    flat = strips[...].reshape(3 * NCY * SPREAD, LANES)
    for phase in range(PHASES):
        pick = jnp.where((phase * LANES + dst) % NZ // BLK == src % NCZ, 1.0, 0.0).astype(BF16)
        got = jnp.dot(flat, pick, preferred_element_type=F32)
        spread[phase] = got.reshape(3, NCY, SPREAD, LANES)

    both = received(SECOND, got_a, got_b, tail_a, tail_b)
    for q in range(WHOLE + 1):
        size = 16 if q < WHOLE else REST
        values = [both(n, q) for n in range(SECOND)]
        for side, rows in ((0, BEFORE), (1, BEYOND)):
            got = [v[side] for v in values]
            for row, value in zip(rows, (got[0] + got[1], got[2], got[3])):
                smooth[plane(smooth, row, q, size), :] = value
            for a, w in enumerate(weights):
                for n, row in enumerate(rows[1:]):
                    w[plane(w, row, q, size), :] = got[4 + 2 * a + n]

    def prolong(t, i, carry):
        n = t // PAIR
        phase = i % PHASES
        here = span(t, 0, PAD)
        total = smooth[here, :]
        for a, w in enumerate(weights):
            if i == PAIR // 2:
                values = jnp.where(
                    lane[0:PAD] < LANES // 2,
                    spread[phase, a, 2 * n, 0:PAD],
                    spread[phase, a, 2 * n + 1, 0:PAD],
                )
            else:
                values = spread[phase, a, 2 * n + (1 if i > PAIR // 2 else 0), 0:PAD]
            total = total + w[here, :] * values
        first[here, :] = total
        return carry

    over_tiles(prolong, 0)
    sweep(first, second, tx, ty, tz, k, b, TOP - 2, OWN + 4)
    sweep(second, first, tx, ty, tz, k, b, TOP - 1, OWN + 2)

    def last(t, i, carry):
        total, after = coupled(first, tx, ty, tz, t, TOP, OWN, carry)
        here = span(t, TOP, OWN)
        out[:, at(t)] = b[here, :] + (1.0 - OMEGA_FINE) * carry[0] + k[here, :] * total
        return after

    over_tiles(last, coupled_start(first, TOP, OWN))


def finish(count, near_rows, far_rows, got_a, got_b, smooth, w0, w1, w2, tx, ty, tz, k, b):
    rows = 2 * count

    def kernel(*refs):
        finish_kernel(count, *refs)

    return pl.pallas_call(
        kernel,
        out_shape=(
            jax.ShapeDtypeStruct((OWN, PLANE), F32),
            jax.ShapeDtypeStruct((2, LANES), F32),
        )
        + (padded(),) * 4,
        in_specs=in_vmem(13),
        out_specs=tuple(in_vmem(6)),
        input_output_aliases={n + 4: n + 2 for n in range(4)},
        scratch_shapes=[vmem((count * ALL_ROWS, LANES))]
        + [
            vmem((4, rows + 2 * EDGE, LANES)),
            vmem((3, rows, LANES)),
            vmem((5, rows + 2 * EDGE, LANES)),
            vmem((5, rows, LANES)),
            vmem((5, rows + 2 * EDGE, LANES)),
            vmem((5, rows, LANES)),
        ]
        + [vmem((rows + 2 * EDGE, LANES))] * 5
        + [
            vmem((3, NCY, SPREAD, LANES), BF16),
            vmem((PHASES, 3, NCY, SPREAD, LANES)),
            padded(),
            padded(),
        ]
        + tails(SECOND),
        compiler_params=params(10 + count // 8),
        cost_estimate=lasting(12),
    )(near_rows, far_rows, got_a, got_b, smooth, w0, w1, w2, tx, ty, tz, k, b)[:2]


def swapped(pay_a, pay_b):
    count = lax.axis_size("gx")
    got_a = lax.ppermute(pay_a, "gx", [(i, i ^ 1) for i in range(count)])
    inner = [(i, i + 1 if i % 2 else i - 1) for i in range(1, count - 1)]
    return got_a, lax.ppermute(pay_b, "gx", inner)


def rounds(count):
    bits = count.bit_length() - 1
    found = []
    while bits >= 4:
        low = 1 << (bits - 2)
        found.append((low, 2 * low, 3 * low))
        bits -= 2
    return found + [(1 << bit,) for bit in reversed(range(bits))]


def arrival(count):
    order = [0]
    for steps in rounds(count):
        order = [distance ^ step for step in (0, *steps) for distance in order]
    return order


def stacked_kernel(*refs):
    out, low = refs[-1], 0
    for ref in refs[:-1]:
        out[low : low + ref.shape[0], :] = ref[...]
        low += ref.shape[0]


def stacked(blocks):
    rows = sum(block.shape[0] for block in blocks)
    return pl.pallas_call(
        stacked_kernel,
        out_shape=vmem((rows, LANES)),
        in_specs=in_vmem(len(blocks)),
        out_specs=in_vmem(1)[0],
        compiler_params=params(4),
    )(*blocks)


def gather(rows):
    count = lax.axis_size("gx")
    for steps in rounds(count):
        blocks = [rows]
        for step in steps:
            blocks.append(lax.ppermute(rows, "gx", [(i, i ^ step) for i in range(count)]))
        if steps != (1,):
            rows = stacked(blocks)
    return blocks


def per_device(
    rhs, accumulation, trans_x, trans_y, trans_z, basis_center, basis_side, coarse_inverse
):
    count = lax.axis_size("gx")
    raw, *own_fields, pay_a, pay_b = prepare(
        rhs, accumulation, trans_x, trans_y, trans_z, basis_center, basis_side
    )
    got_a, got_b = swapped(pay_a, pay_b)
    operator = assemble(*own_fields, coarse_inverse)
    *own_fields, k, b, smooth, edges, pay_a, pay_b = presmooth(
        got_a, got_b, raw, *own_fields, operator
    )
    got_a, got_b = swapped(pay_a, pay_b)
    part = restrict(smooth, raw, *own_fields, edges, operator)
    near_rows, far_rows = gather(part)
    tx, ty, tz, dg, w0, w1, w2 = own_fields
    return finish(
        count, near_rows, far_rows, got_a, got_b, smooth, w0, w1, w2, tx, ty, tz, k, b
    )


def solution(mesh):
    both = ("grp", "gx")
    cells = P(both, None)
    return jax.shard_map(
        per_device,
        mesh=mesh,
        in_specs=(cells,) * 6 + (P(None, both, None), cells),
        out_specs=(cells, cells),
        check_vma=False,
    )
```

```python
import jax
import jax.numpy as jnp
from jax import lax
from jax.experimental import pallas as pl
from jax.experimental.pallas import tpu as pltpu
from jax.sharding import PartitionSpec as P

BLK = 10
NCY = 8
NCZ = 16
CSW = 6
NZ = 160
PLANE = 12800
COARSE = NCY * NCZ
OMEGA_FINE = 0.7
OMEGA_COARSE = 0.6

LANES = 128
TILES = PLANE // LANES
PHASES = 5
PAIR = 25
PAIRS = TILES // PAIR
OWN = 20
TOP = 3
PAD = OWN + 2 * TOP
HEAD = (TOP, TOP + 1, TOP + 2)
LAST = (TOP + OWN - 1, TOP + OWN - 2, TOP + OWN - 3)
BEFORE = (TOP - 1, TOP - 2, TOP - 3)
BEYOND = (TOP + OWN, TOP + OWN + 1, TOP + OWN + 2)
SPREAD = 32
GROUP = 20
QUARTERS = 4
LT = QUARTERS * NZ // LANES
PAIRED = ((0, 0), (0, 1), (0, 2), (1, 1), (1, 2), (2, 2))
FIRST = 12
SECOND = 15
WHOLE = TILES // 16
REST = TILES % 16
OFFSET = (0, -1, 1)
SAME = ((0, 0), (0, 1), (0, 2), (0, 3), (1, 1), (1, 2), (1, 3), (2, 2), (2, 3), (3, 3), (1, 4), (2, 4), (3, 4))
ACROSS = tuple((u, v) for u in range(4) for v in range(4) if abs(u - v) <= 2)
Y_ROW = len(SAME)
Z_ROW = Y_ROW + len(ACROSS)
INVERSE_ROW = Z_ROW + len(ACROSS)
RHS_ROW = INVERSE_ROW + 2
ALL_ROWS = 56
EDGES = 24
F32 = jnp.float32
BF16 = jnp.bfloat16


def params(mib):
    return pltpu.CompilerParams(vmem_limit_bytes=mib << 20)


def lasting(microseconds):
    return pl.CostEstimate(
        flops=0, transcendentals=0, bytes_accessed=int(3.5e6 * microseconds)
    )


def vmem(shape, dtype=F32):
    return pltpu.VMEM(shape, dtype)


def in_vmem(count):
    return [pl.BlockSpec(memory_space=pltpu.VMEM)] * count


def in_hbm(count):
    return [pl.BlockSpec(memory_space=pltpu.HBM)] * count


def padded():
    return vmem((TILES * PAD + 8, LANES))


def padded_out():
    return pltpu.HBM((TILES * PAD + 8, LANES), F32)


def cells(dtype=BF16):
    return vmem((OWN, PLANE), dtype)


def semaphores(*shape):
    return pltpu.SemaphoreType.DMA(shape)


def stream(sources, buffers, sems):
    width = PLANE // PAIRS

    def copy(field, n):
        lanes = pl.ds(pl.multiple_of(n * width, width), width)
        return pltpu.make_async_copy(
            sources[field].at[:, lanes], buffers[field].at[:, lanes], sems.at[field, n]
        )

    for n in range(PAIRS):
        for field in range(len(sources)):
            copy(field, n).start()

    def wait(n):
        for field in range(len(sources)):
            copy(field, n).wait()

    return wait


def copies(sources, targets, sems):
    made = [
        pltpu.make_async_copy(src, dst, sems.at[n])
        for n, (src, dst) in enumerate(zip(sources, targets))
    ]
    for copy in made:
        copy.start()
    return made


def lane_roll(value, steps):
    return pltpu.roll(value, steps % LANES, 1)


def lanes_of(rows):
    return lax.broadcasted_iota(jnp.int32, (rows, LANES), 1)


def rows_of(rows):
    return lax.broadcasted_iota(jnp.int32, (rows, LANES), 0)


def at(t):
    return pl.ds(pl.multiple_of(t * LANES, LANES), LANES)


def span(t, low, count):
    return pl.ds(t * PAD + low, count)


def own(ref, t):
    return ref[:, at(t)].astype(F32)


def over_tiles(body, carry, before=None, unroll=1):
    def step(n, carry):
        if before is not None:
            before(n)
        for i in range(PAIR):
            carry = body(n * PAIR + i, i, carry)
        return carry

    return lax.fori_loop(0, PAIRS, step, carry, unroll=unroll)


def z_blocks(phase, lane_side):
    cell = lax.broadcasted_iota(jnp.int32, (LANES, LANES), lane_side) + phase * LANES % NZ
    cell = jnp.where(cell >= NZ, cell - NZ, cell)
    first = lax.broadcasted_iota(jnp.int32, (LANES, LANES), 1 - lane_side)
    first = (first % NCZ if lane_side else first) * BLK
    return jnp.where((cell >= first) & (cell < first + BLK), 1.0, 0.0).astype(BF16)


def halves(value):
    high = value.astype(BF16)
    low = (value - high.astype(F32)).astype(BF16)
    return high, low


def remainder(value):
    return value - value.astype(BF16).astype(F32)


def parity():
    return lax.rem(lax.axis_index("gx"), 2)


def coupled(src, tx, ty, tz, t, low, count, carry):
    center, following, turned, y_next, z_flux, y_flux, y_flux_before = carry
    lane = lanes_of(count)
    here = span(t, low, count)
    second = src[span(jnp.minimum(t + 2, TILES - 1), low, count), :]
    turned_next = lane_roll(following, -1)
    z_up = jnp.where(lane == LANES - 1, turned_next, turned)
    y_second = lane_roll(second, -(NZ - LANES))
    y_up = jnp.where(lane >= 2 * LANES - NZ, y_second, y_next)
    tz_t = tz[here, :]
    ty_t = ty[here, :]
    z_flux_new = lane_roll(tz_t * center, 1)
    z_down = jnp.where(lane == 0, z_flux, z_flux_new)
    y_down = jnp.where(lane < NZ - LANES, y_flux_before, y_flux)
    y_flux_new = lane_roll(ty_t * center, NZ - LANES)
    total = tz_t * z_up + z_down
    total = total + (ty_t * y_up + y_down)
    total = total + tx[here, :] * src[span(t, low + 1, count), :]
    total = total + tx[span(t, low - 1, count), :] * src[span(t, low - 1, count), :]
    return total, (following, second, turned_next, y_second, z_flux_new, y_flux_new, y_flux)


def coupled_start(src, low, count):
    center = src[span(0, low, count), :]
    following = src[span(1, low, count), :]
    zero = center * 0.0
    turned = lane_roll(center, -1)
    return center, following, turned, lane_roll(following, -(NZ - LANES)), zero, zero, zero


def sweep(src, dst, tx, ty, tz, k, b, low, count):
    def body(t, i, carry):
        total, after = coupled(src, tx, ty, tz, t, low, count, carry)
        here = span(t, low, count)
        dst[here, :] = b[here, :] + (1.0 - OMEGA_FINE) * carry[0] + k[here, :] * total
        return after

    over_tiles(body, coupled_start(src, low, count), unroll=4)


def plane(ref, row, q, size, stride=PAD):
    return pl.ds(16 * q * stride + row, size, stride)


def read_plane(ref, row, stride=PAD):
    return lambda q, size: ref[plane(ref, row, q, size, stride), :]


def send_both(pay_a, pay_b, tail_a, tail_b, right, left):
    even = parity() == 0
    count = len(right)
    for n in range(count):
        for q in range(WHOLE + 1):
            size = 16 if q < WHOLE else REST
            r, l = right[n](q, size), left[n](q, size)
            a, b = jnp.where(even, r, l), jnp.where(even, l, r)
            if q < WHOLE:
                rows = slice((n * WHOLE + q) * 16, (n * WHOLE + q) * 16 + 16)
                pay_a[rows, :] = a.astype(BF16)
                pay_b[rows, :] = b.astype(BF16)
            else:
                rows = slice(n * REST, n * REST + REST)
                tail_a[rows, :] = a
                tail_b[rows, :] = b
    pay_a[count * WHOLE * 16 :, :] = tail_a[...].astype(BF16)
    pay_b[count * WHOLE * 16 :, :] = tail_b[...].astype(BF16)


def received(count, got_a, got_b, tail_a, tail_b):
    even = parity() == 0
    tail_a[...] = got_a[count * WHOLE * 16 :, :].astype(F32)
    tail_b[...] = got_b[count * WHOLE * 16 :, :].astype(F32)

    def both(n, q):
        if q < WHOLE:
            rows = slice((n * WHOLE + q) * 16, (n * WHOLE + q) * 16 + 16)
            a, b = got_a[rows, :].astype(F32), got_b[rows, :].astype(F32)
        else:
            rows = slice(n * REST, n * REST + REST)
            a, b = tail_a[rows, :], tail_b[rows, :]
        return jnp.where(even, b, a), jnp.where(even, a, b)

    return both


def payload_rows(count):
    return -(-count * TILES // 16) * 16


def payload(count):
    return jax.ShapeDtypeStruct((payload_rows(count), LANES), BF16)


def tails(count):
    return [vmem((payload_rows(count) - count * WHOLE * 16, LANES))] * 2


def low_part(f):
    return lambda q, size: remainder(f(q, size))


def prepare_kernel(
    rhs_in, accum_in, x_in, y_in, z_in, center_in, side_in,
    raw, tx_n, ty_n, tz_n, dg_n, w0_n, w1_n, w2_n, pay_a, pay_b,
    rhs_v, accum_v, x_v, y_v, z_v, center_v, lower_v, upper_v, tail_a, tail_b, sems,
):
    wait = stream(
        (rhs_in, accum_in, x_in, y_in, z_in, center_in, side_in.at[0], side_in.at[1]),
        (rhs_v, accum_v, x_v, y_v, z_v, center_v, lower_v, upper_v),
        sems,
    )
    weights = (w0_n, w1_n, w2_n)
    lane = lanes_of(OWN)

    def load(t, i, carry):
        z_before, y_before, y_second = carry
        for ref, src in zip(weights, (center_v, lower_v, upper_v)):
            ref[span(t, TOP, OWN), :] = own(src, t)
        z_pos = (i * LANES + lane) % NZ
        cells = t * LANES + lane
        here = span(t, TOP, OWN)
        x, y, z = own(x_v, t), own(y_v, t), own(z_v, t)
        y_inner = jnp.where(cells < PLANE - NZ, y, 0.0)
        z_inner = jnp.where(z_pos != NZ - 1, z, 0.0)
        z_rolled = lane_roll(z_inner, 1)
        y_rolled = lane_roll(y_inner, NZ - LANES)
        tx_n[span(t, TOP - 1, 1), :] = jnp.zeros((1, LANES), F32)
        tx_n[here, :] = x
        ty_n[here, :] = y_inner
        tz_n[here, :] = z_inner
        total = own(accum_v, t) + x + tx_n[span(t, TOP - 1, OWN), :]
        total = total + y + jnp.where(lane < NZ - LANES, y_second, y_before)
        total = total + z + jnp.where(lane == 0, z_before, z_rolled)
        dg_n[here, :] = total
        raw[here, :] = rhs_v[:, at(t)]
        return z_rolled, y_rolled, y_before

    zero = lanes_of(OWN).astype(F32) * 0.0
    over_tiles(load, (zero, zero, zero), wait)

    def first_sweep(row):
        r, d = read_plane(raw, row), read_plane(dg_n, row)
        return lambda q, size: OMEGA_FINE * r(q, size) / d(q, size)

    def planes(rows):
        near, second, _ = rows
        r, d = read_plane(raw, near), read_plane(dg_n, near)
        found = [r, low_part(r), d, low_part(d)]
        found += [read_plane(ty_n, near), read_plane(tz_n, near), first_sweep(second)]
        found += [read_plane(tx_n, row) for row in rows[:2]]
        return found + [read_plane(w, near) for w in weights]

    right, left = LAST, HEAD
    send_both(pay_a, pay_b, tail_a, tail_b, planes(right), planes(left))


def prepare(*fields):
    return pl.pallas_call(
        prepare_kernel,
        out_shape=(padded(),) * 8 + (payload(FIRST),) * 2,
        in_specs=in_hbm(7),
        out_specs=tuple(in_vmem(10)),
        scratch_shapes=[cells(F32)] + [cells()] * 7 + tails(FIRST) + [semaphores(8, PAIRS)],
        compiler_params=params(46),
        cost_estimate=lasting(6),
    )(*fields)


def add_share(shares, u, v, value):
    pair = (min(u, v), max(u, v))
    shares[pair] = shares[pair] + value if pair in shares else value


def add_face(shares, u, v, value):
    add_share(shares, u, v, -2.0 * value if u == v else -value)


def presmooth_kernel(
    got_a, got_b, raw, tx_in, ty_in, tz_in, dg_in, w0_in, w1_in, w2_in, operator,
    tx, ty, tz, dg, w0, w1, w2,
    k, b, smooth, part, pay_a, pay_b,
    work, tail_a, tail_b, second_a, second_b, edges, sums, rest, shares_v,
):
    weights = (w0, w1, w2)
    both = received(FIRST, got_a, got_b, tail_a, tail_b)
    for q in range(WHOLE + 1):
        size = 16 if q < WHOLE else REST

        def put(ref, row, value):
            ref[plane(ref, row, q, size), :] = value

        def get(ref, row):
            return ref[plane(ref, row, q, size), :]

        values = [both(n, q) for n in range(FIRST)]
        left, right = [v[0] for v in values], [v[1] for v in values]
        for got, rows in ((left, BEFORE), (right, BEYOND)):
            put(b, rows[0], got[0] + got[1])
            put(ty, rows[0], got[4])
            put(tz, rows[0], got[5])
            put(b, rows[1], got[6])
            put(tx, rows[0], got[7])
            put(tx, rows[1], got[8])
            for a, w in enumerate(weights):
                put(w, rows[0], got[9 + a])
        tx_before = left[7]
        tx_last = get(tx, LAST[0])
        beyond = right[2] + right[3]
        put(dg, BEFORE[0], left[2] + left[3])
        put(dg, BEYOND[0], jnp.where(beyond > 0.0, beyond + tx_last, 0.0))
        put(dg, HEAD[0], get(dg, HEAD[0]) + tx_before)
        first = [get(w, HEAD[0]) for w in weights]
        last = [get(w, LAST[0]) for w in weights]
        from_next = [right[9 + a] for a in range(3)]
        products = [tx_last * last[a] * from_next[c] for a in range(3) for c in range(3)]
        products += [tx_before * first[a] * first[c] for a, c in PAIRED]
        for n, value in enumerate(products):
            edges[plane(edges, n, q, size, EDGES), :] = value

    def scale(t, i, carry):
        here = span(t, TOP - 1, OWN + 2)
        for row in (TOP - 1, TOP + OWN):
            smooth[span(t, row, 1), :] = jnp.zeros((1, LANES), F32)
        diag = dg[here, :]
        value = jnp.where(diag > 0.0, OMEGA_FINE / diag, 0.0)
        k[here, :] = value
        b[span(t, TOP, OWN), :] = raw[span(t, TOP, OWN), :]
        b[here, :] = value * b[here, :]
        return carry

    over_tiles(scale, 0, unroll=4)
    sweep(b, work, tx, ty, tz, k, b, TOP - 1, OWN + 2)
    sweep(work, smooth, tx, ty, tz, k, b, TOP, OWN)
    for q in range(WHOLE + 1):
        size = 16 if q < WHOLE else REST
        last = tx[plane(tx, LAST[0], q, size), :] * smooth[plane(smooth, LAST[0], q, size), :]
        first = tx[plane(tx, BEFORE[0], q, size), :] * smooth[plane(smooth, HEAD[0], q, size), :]
        values = [last * w[plane(w, BEYOND[0], q, size), :] for w in weights]
        values += [first * w[plane(w, BEFORE[0], q, size), :] for w in weights]
        values += [jnp.zeros((size, LANES), F32)] * 3
        for n, value in enumerate(values):
            edges[plane(edges, 15 + n, q, size, EDGES), :] = value

    def planes(rows):
        near = read_plane(smooth, rows[0])
        found = [near, low_part(near), read_plane(smooth, rows[1]), read_plane(smooth, rows[2])]
        found += [read_plane(w, row) for w in weights for row in rows[1:]]
        found += [read_plane(ref, rows[1]) for ref in (raw, dg, ty, tz)]
        return found + [read_plane(tx, rows[2])]

    send_both(pay_a, pay_b, second_a, second_b, planes(LAST), planes(HEAD))

    rows = 48 + EDGES
    lane = lanes_of(rows)
    row8 = rows_of(8)
    for n in range(PAIR):
        rest[n * 24 + 16 : n * 24 + 24, :] = jnp.zeros((8, LANES), F32)

    def residual(t, i, carry):
        total, following = coupled(smooth, tx, ty, tz, t, TOP, OWN, carry)
        rest[i * 24 : i * 24 + OWN, :] = (
            raw[span(t, TOP, OWN), :] - dg[span(t, TOP, OWN), :] * carry[0] + total
        )
        left_over = rest[i * 24 : i * 24 + 24, :]
        folded = []
        for w in weights:
            f = w[span(t, TOP, 24), :] * left_over
            mixed = jnp.where(row8 < BLK - 8, f[8:16], 0.0)
            folded += [f[0:8] + mixed, jnp.where(row8 < 4, f[16:24], 0.0) + (f[8:16] - mixed)]
        for n, value in enumerate(folded):
            shares_v[pl.ds(t * rows + 8 * n, 8), :] = value
        shares_v[pl.ds(t * rows + 48, EDGES), :] = edges[pl.ds(t * EDGES, EDGES), :]
        return following

    over_tiles(residual, coupled_start(smooth, TOP, OWN), unroll=4)

    def strips(n, carry):
        for strip in range(2):
            for phase in range(PHASES):
                total = None
                for i in range(phase, PAIR, PHASES):
                    if strip == 0 and i > PAIR // 2 or strip == 1 and i < PAIR // 2:
                        continue
                    value = shares_v[pl.ds((n * PAIR + i) * rows, rows), :]
                    if i == PAIR // 2:
                        value = jnp.where((lane < LANES // 2) == (strip == 0), value, 0.0)
                    total = value if total is None else total + value
                sums[phase, 2 * n + strip] = total
        return carry

    lax.fori_loop(0, PAIRS, strips, 0)

    found = jnp.zeros((NCY * (48 + EDGES), LANES), F32)
    for phase in range(PHASES):
        pick = z_blocks(phase, 0)
        pieces = halves(sums[phase].reshape(NCY * (48 + EDGES), LANES))
        found = found + jnp.dot(
            jnp.concatenate(pieces, axis=1),
            jnp.concatenate([pick, pick], axis=0),
            preferred_element_type=F32,
        )
    placed = found[0:rows]
    for strip in range(1, NCY):
        placed = placed + lane_roll(found[strip * rows : strip * rows + rows], strip * NCZ)
    shares = {}
    for n, (a, c) in enumerate(PAIRED):
        add_share(shares, 1 + OFFSET[a], 1 + OFFSET[c], placed[57 + n : 58 + n])
    for a in range(3):
        for c in range(3):
            add_face(shares, 2 + OFFSET[a], 3 + OFFSET[c], placed[48 + 3 * a + c : 49 + 3 * a + c])
    part[0:ALL_ROWS, :] = operator[...]
    for n, pair in enumerate(SAME):
        if pair in shares:
            part[n : n + 1, :] += shares[pair]
    for a in range(3):
        for block in range(2):
            row = RHS_ROW + 2 + block + OFFSET[a]
            low = (2 * a + block) * 8
            part[row : row + 1, :] += jnp.sum(placed[low : low + 8], axis=0, keepdims=True)
        for low, u in ((63, 3), (66, 0)):
            row = RHS_ROW + 1 + u + OFFSET[a]
            part[row : row + 1, :] += placed[low + a : low + a + 1]


def presmooth(got_a, got_b, raw, tx, ty, tz, dg, w0, w1, w2, operator):
    return pl.pallas_call(
        presmooth_kernel,
        out_shape=(padded(),) * 10 + (vmem((ALL_ROWS, LANES)),) + (payload(SECOND),) * 2,
        in_specs=in_vmem(11),
        out_specs=tuple(in_vmem(13)),
        input_output_aliases={n + 3: n for n in range(7)},
        scratch_shapes=[padded()]
        + tails(FIRST)
        + tails(SECOND)
        + [
            vmem((TILES * EDGES, LANES)),
            vmem((PHASES, NCY, 48 + EDGES, LANES)),
            vmem((PAIR * 24, LANES)),
            vmem((TILES * (48 + EDGES), LANES)),
        ],
        compiler_params=params(14),
        cost_estimate=lasting(8),
    )(got_a, got_b, raw, tx, ty, tz, dg, w0, w1, w2, operator)


def regrouped(ref, dst, shift, index, load, cut=False):
    lane = lanes_of(OWN)
    rolled = {}

    def piece(quarter, t):
        offset = 3200 * quarter + NZ * shift - NZ * quarter
        first, turn = (t * LANES + offset) // LANES, offset % LANES

        def source(tile):
            tile = min(max(tile, 0), TILES - 1)
            key = (tile, turn)
            if key not in rolled:
                value = load(ref, tile)
                rolled[key] = lane_roll(value, -turn) if turn else value
            return rolled[key]

        if quarter * GROUP + shift < 0 or quarter * GROUP + shift >= 4 * GROUP:
            return None
        low_lane, high_lane = max(0, quarter * NZ - t * LANES), min(LANES, (quarter + 1) * NZ - t * LANES)
        if turn == 0 or high_lane <= LANES - turn:
            return source(first)
        if low_lane >= LANES - turn:
            return source(first + 1)
        return jnp.where(lane < LANES - turn, source(first), source(first + 1))

    for t in range(LT):
        first = t * LANES // NZ
        last = (t * LANES + LANES - 1) // NZ
        value = piece(first, t)
        if last != first:
            other = piece(last, t)
            value = jnp.zeros((OWN, LANES), F32) if value is None else value
            other = jnp.zeros((OWN, LANES), F32) if other is None else other
            value = jnp.where(lane < last * NZ - t * LANES, value, other)
        elif value is None:
            value = jnp.zeros((OWN, LANES), F32)
        if cut:
            value = jnp.where(rows_of(OWN) < OWN - 1, value, 0.0)
        dst[index, t, 0:OWN, :] = value
        if index >= BLK:
            dst[index - BLK, t, OWN : OWN + 4, :] = value[16:OWN]
        else:
            dst[index, t, 24:SPREAD, :] = jnp.zeros((SPREAD - 24, LANES), F32)


def assemble_kernel(
    tx_n, ty_n, tz_n, dg_n, w0_n, w1_n, w2_n, inverse, out,
    w, tx, ty, tz, dg, fields, rows_in, found,
):
    weights = (w0_n, w1_n, w2_n)

    def plain(ref, tile):
        return ref[tile * PAD + TOP : tile * PAD + TOP + OWN, :]

    for g in range(GROUP):
        regrouped(tx_n, tx, g, g, plain, cut=True)
        regrouped(ty_n, ty, g, g, plain)
        regrouped(tz_n, tz, g, g, plain)
        regrouped(dg_n, dg, g, g, plain)
    for g in range(GROUP + 1):
        for a, weight in enumerate(weights):
            regrouped(weight, w.at[a], g, g, plain)

    lane8 = lanes_of(8)

    def combo(index, carry):
        shared = index >= 4 * LT
        half = jnp.where(shared, 0, index // (2 * LT))
        t = jnp.where(shared, index - 4 * LT, index // 2 % LT)
        low = jnp.where(shared, 16, index % 2 * 8)
        t_next = jnp.minimum(t + 1, LT - 1)
        same = pl.ds(pl.multiple_of(low, 8), 8)
        after = pl.ds(low + 1, 8)
        d_sum = [None] * 6
        x_sum = [None] * 9
        z_sum = [None] * 9
        for step in range(BLK):
            g = half * BLK + step
            here = [w[a, g, t, same, :] for a in range(3)]
            x_up = [w[a, g, t, after, :] for a in range(3)]
            y_up = [w[a, g + 1, t, same, :] for a in range(3)]
            z_up = [
                jnp.where(
                    lane8 == LANES - 1,
                    lane_roll(w[a, g, t_next, same, :], -1),
                    lane_roll(here[a], -1),
                )
                for a in range(3)
            ]
            d_t, x_t = dg[g, t, same, :], tx[g, t, same, :]
            y_t, z_t = ty[g, t, same, :], tz[g, t, same, :]
            d_w = [d_t * v for v in here]
            x_w = [x_t * v for v in here]
            y_w = [y_t * v for v in here]
            z_w = [z_t * v for v in here]
            for n, (a, c) in enumerate(PAIRED):
                term = d_w[a] * here[c]
                if step < BLK - 1:
                    cross = y_w[a] * y_up[c]
                    cross = cross + (cross if a == c else y_w[c] * y_up[a])
                    term = term - cross
                d_sum[n] = term if d_sum[n] is None else d_sum[n] + term
            for a in range(3):
                for c in range(3):
                    n = 3 * a + c
                    x_term = x_w[a] * x_up[c]
                    z_term = z_w[a] * z_up[c]
                    x_sum[n] = x_term if x_sum[n] is None else x_sum[n] + x_term
                    z_sum[n] = z_term if z_sum[n] is None else z_sum[n] + z_term
                    if step == BLK - 1:
                        fields[24 + n, half, t, same, :] = y_w[a] * y_up[c]
        for n in range(6):
            fields[n, half, t, same, :] = d_sum[n]
        for n in range(9):
            fields[6 + n, half, t, same, :] = x_sum[n]
            fields[15 + n, half, t, same, :] = z_sum[n]
        return carry

    lax.fori_loop(0, 5 * LT, combo, 0)

    row8 = rows_of(8)

    def fold(index, carry):
        half = index // LT
        t = index % LT
        cols = pl.ds(pl.multiple_of(half * LANES, LANES), LANES)

        mine = (row8 < 4) == (half == 0)

        def tiles_of(n):
            found = [fields[n, half, t, 8 * s : 8 * s + 8, :] for s in range(2)]
            return found + [jnp.where(mine, fields[n, 0, t, 16:24, :], 0.0)]

        def blocks(v, first):
            return (
                v[0] + jnp.where(row8 < first, v[1], 0.0),
                jnp.where(row8 >= 2, v[1], 0.0) + v[2],
            )

        x_tiles = [tiles_of(6 + n) for n in range(9)]
        x_in = [blocks(v, 1) for v in x_tiles]
        for n, (a, c) in enumerate(PAIRED):
            both = blocks(tiles_of(n), 2)
            for s in range(2):
                value = both[s] - x_in[3 * a + c][s] - x_in[3 * c + a][s]
                rows_in[t, 16 * n + 8 * s : 16 * n + 8 * s + 8, cols] = value
        for n in range(9):
            rows_in[t, 96 + 8 * n : 104 + 8 * n, cols] = jnp.where(row8 == 1, x_tiles[n][1], 0.0)
            for first, base in ((24, 168), (15, 312)):
                both = blocks(tiles_of(first + n), 2)
                for s in range(2):
                    low = base + 16 * n + 8 * s
                    rows_in[t, low : low + 8, cols] = both[s]
        return carry

    lax.fori_loop(0, 2 * LT, fold, 0)

    coarse = lanes_of(8)
    first = coarse // (2 * NCZ) * NZ + coarse % NCZ * BLK
    first = jnp.concatenate(
        [jnp.where(coarse // NCZ % 2 == half, first, -NZ) for half in range(2) for _ in range(NCZ)],
        axis=0,
    )
    place = jnp.concatenate([rows_of(LANES)] * 2, axis=0)
    total = jnp.zeros((456, 2 * LANES), F32)
    for t in range(LT):
        step = place + t * LANES - first
        inside = jnp.where((step >= 0) & (step < BLK - 1), 1.0, 0.0)
        crossing = jnp.where(step == BLK - 1, 1.0, 0.0)
        pick = jnp.concatenate([inside, crossing], axis=1).astype(BF16)
        for piece in halves(rows_in[t]):
            total = total + jnp.dot(piece, pick, preferred_element_type=F32)
    found[0:57, :] = jnp.sum(total.reshape(57, 8, 2 * LANES), axis=1)

    def both(row):
        return found[row : row + 1, 0:LANES] + found[row : row + 1, LANES:]

    def inside(row):
        return found[row : row + 1, 0:LANES]

    def crossing(row):
        return found[row : row + 1, LANES:]

    shares, y_shares, z_shares = {}, {}, {}
    for block in range(2):
        rows = [1 + block + OFFSET[a] for a in range(3)]
        for n, (a, c) in enumerate(PAIRED):
            value = both(2 * n + block)
            value = value - inside(39 + 2 * (3 * a + c) + block) - inside(39 + 2 * (3 * c + a) + block)
            add_share(shares, rows[a], rows[c], value)
        for a in range(3):
            for c in range(3):
                n = 3 * a + c
                pair = (rows[a], rows[c])
                for kept, value in (
                    (y_shares, both(21 + 2 * n + block)),
                    (z_shares, crossing(39 + 2 * n + block)),
                ):
                    kept[pair] = kept[pair] - value if pair in kept else -value
                if block == 0:
                    add_face(shares, 1 + OFFSET[a], 2 + OFFSET[c], both(12 + n))
    out[...] = jnp.zeros_like(out)
    for first, pairs, kept in ((0, SAME, shares), (Y_ROW, ACROSS, y_shares), (Z_ROW, ACROSS, z_shares)):
        for n, pair in enumerate(pairs):
            if pair in kept:
                out[first + n : first + n + 1, :] = kept[pair]
    out[INVERSE_ROW : INVERSE_ROW + 2, :] = inverse[...]


def assemble(tx, ty, tz, dg, w0, w1, w2, inverse):
    slab = (LT, SPREAD, LANES)
    return pl.pallas_call(
        assemble_kernel,
        out_shape=vmem((ALL_ROWS, LANES)),
        in_specs=in_vmem(8),
        out_specs=in_vmem(1)[0],
        scratch_shapes=[
            vmem((3, GROUP + 1) + slab),
            vmem((GROUP,) + slab),
            vmem((GROUP,) + slab),
            vmem((GROUP,) + slab),
            vmem((GROUP,) + slab),
            vmem((33, 2, LT, 24, LANES)),
            vmem((LT, 456, 2 * LANES)),
            vmem((57, 2 * LANES)),
        ],
        compiler_params=params(24),
        cost_estimate=lasting(10),
    )(tx, ty, tz, dg, w0, w1, w2, inverse)


EDGE = 8


def coarse_solve(count, halves_in, gathered, same, same_t, y_mat, y_mat_t, z_mat, z_mat_t, inv, rhs, e, e_y, e_z):
    rows = 2 * count
    here = pl.ds(EDGE, rows)
    for ref in (same, y_mat, z_mat, inv, rhs, e, e_y, e_z):
        ref[...] = jnp.zeros_like(ref)
    index = lax.axis_index("gx")
    for n, distance in enumerate(arrival(count)):
        ref, n = halves_in[n // (count // 2)], n % (count // 2)
        place = pl.multiple_of(lax.bitwise_xor(index, distance) * ALL_ROWS, ALL_ROWS)
        gathered[pl.ds(place, ALL_ROWS), :] = ref[n * ALL_ROWS : n * ALL_ROWS + ALL_ROWS, :]

    def share(row):
        return gathered[pl.ds(row, count, ALL_ROWS), :]

    def add(ref, u, value):
        place = pl.ds(EDGE - 1 + u, count, 2)
        ref[place, :] = ref[place, :] + value

    for n, (u, v) in enumerate(SAME):
        add(same.at[v - u], u, share(n))
    for n, (u, v) in enumerate(ACROSS):
        add(y_mat.at[v - u + 2], u, share(Y_ROW + n))
        add(z_mat.at[v - u + 2], u, share(Z_ROW + n))
    for u in range(-1, 5):
        add(rhs, u, share(RHS_ROW + 1 + u))
    for block in range(2):
        inv[pl.ds(EDGE + block, count, 2), :] = OMEGA_COARSE * share(INVERSE_ROW + block)
    for step in range(1, 4):
        same_t[step - 1] = same[step, pl.ds(EDGE - step, rows), :]
    for step in range(-2, 3):
        y_mat_t[step + 2] = y_mat[step + 2, pl.ds(EDGE - step, rows), :]
        z_mat_t[step + 2] = z_mat[step + 2, pl.ds(EDGE - step, rows), :]
    e[here, :] = inv[here, :] * rhs[here, :]

    def one(index, carry):
        at_step = {step: e[pl.ds(EDGE + step, rows), :] for step in range(-3, 4)}
        e_y[here, :] = lane_roll(at_step[0], -NCZ)
        e_z[here, :] = lane_roll(at_step[0], -1)
        image = same[0, here, :] * at_step[0]
        for step in range(1, 4):
            image = image + same[step, here, :] * at_step[step] + same_t[step - 1] * at_step[-step]
        y_back = z_back = None
        for step in range(-2, 3):
            y_term = y_mat_t[step + 2] * at_step[-step]
            z_term = z_mat_t[step + 2] * at_step[-step]
            y_back = y_term if y_back is None else y_back + y_term
            z_back = z_term if z_back is None else z_back + z_term
        image = image + lane_roll(y_back, NCZ) + lane_roll(z_back, 1)
        for step in range(-2, 3):
            place = pl.ds(EDGE + step, rows)
            image = image + y_mat[step + 2, here, :] * e_y[place, :]
            image = image + z_mat[step + 2, here, :] * e_z[place, :]
        e[here, :] = at_step[0] + inv[here, :] * (rhs[here, :] - image)
        return carry

    lax.fori_loop(0, CSW - 1, one, 0)


def finish_kernel(
    count, near_rows, far_rows, got_a, got_b,
    smooth_in, w0_in, w1_in, w2_in, tx_in, ty_in, tz_in, k_in, b_in,
    out, update, smooth, w0, w1, w2, tx, ty, tz, k, b,
    result, own_update, out_sems, gathered, same, same_t, y_mat, y_mat_t, z_mat, z_mat_t, inv, rhs, e, e_y, e_z, strips, spread, first, second, tail_a, tail_b,
):
    weights = (w0, w1, w2)
    coarse_solve(
        count, (near_rows, far_rows), gathered, same, same_t, y_mat, y_mat_t, z_mat, z_mat_t, inv, rhs, e, e_y, e_z
    )
    base = EDGE + 2 * lax.axis_index("gx")
    own_update[...] = e[pl.ds(base, 2), :]
    sent = pltpu.make_async_copy(own_update, update, out_sems.at[TILES // PHASES])
    sent.start()
    near = {s: e[pl.ds(base + s, 1), :] for s in range(-2, 4)}
    row = rows_of(SPREAD)
    lane = lanes_of(SPREAD)
    for a, s in enumerate((0, -1, 1)):
        value = jnp.where(row < TOP + BLK, near[s], near[s + 1])
        value = jnp.where(row < TOP, near[s - 1], value)
        value = jnp.where(row >= TOP + OWN, near[s + 2], value)
        high = value.astype(BF16).astype(F32)
        rest = value - high
        low = rest.astype(BF16).astype(F32)
        rest = rest - low
        for strip in range(NCY):
            turned = lane_roll(high, -strip * NCZ)
            turned = jnp.where(lane < NCZ, turned, lane_roll(low, (1 - strip) * NCZ))
            turned = jnp.where(lane < 2 * NCZ, turned, lane_roll(rest, (2 - strip) * NCZ))
            turned = jnp.where(lane < 3 * NCZ, turned, 0.0)
            strips[a, strip] = turned.astype(BF16)
    flat = strips[...].reshape(3 * NCY * SPREAD, LANES)
    for phase in range(PHASES):
        pick = z_blocks(phase, 1)
        got = jnp.dot(flat, pick, preferred_element_type=F32)
        spread[phase] = got.reshape(3, NCY, SPREAD, LANES)

    both = received(SECOND, got_a, got_b, tail_a, tail_b)
    for q in range(WHOLE + 1):
        size = 16 if q < WHOLE else REST
        values = [both(n, q) for n in range(SECOND)]
        for side, rows in ((0, BEFORE), (1, BEYOND)):
            got = [v[side] for v in values]
            for row, value in zip(rows, (got[0] + got[1], got[2], got[3])):
                smooth[plane(smooth, row, q, size), :] = value
            for a, w in enumerate(weights):
                for n, row in enumerate(rows[1:]):
                    w[plane(w, row, q, size), :] = got[4 + 2 * a + n]
            scale = jnp.where(got[11] > 0.0, OMEGA_FINE / got[11], 0.0)
            for ref, value in ((k, scale), (b, scale * got[10]), (ty, got[12]), (tz, got[13])):
                ref[plane(ref, rows[1], q, size), :] = value
            if side == 0:
                tx[plane(tx, rows[2], q, size), :] = got[14]

    def prolong(t, i, carry):
        n = t // PAIR
        phase = i % PHASES
        here = span(t, 0, PAD)
        total = smooth[here, :]
        for a, w in enumerate(weights):
            if i == PAIR // 2:
                values = jnp.where(
                    lane[0:PAD] < LANES // 2,
                    spread[phase, a, 2 * n, 0:PAD],
                    spread[phase, a, 2 * n + 1, 0:PAD],
                )
            else:
                values = spread[phase, a, 2 * n + (1 if i > PAIR // 2 else 0), 0:PAD]
            total = total + w[here, :] * values
        first[here, :] = total
        return carry

    over_tiles(prolong, 0)
    sweep(first, second, tx, ty, tz, k, b, TOP - 2, OWN + 4)
    sweep(second, first, tx, ty, tz, k, b, TOP - 1, OWN + 2)

    def last(t, i, carry):
        total, after = coupled(first, tx, ty, tz, t, TOP, OWN, carry)
        here = span(t, TOP, OWN)
        result[:, at(t)] = b[here, :] + (1.0 - OMEGA_FINE) * carry[0] + k[here, :] * total
        if i % PHASES == PHASES - 1:
            part_out(t // PHASES).start()
        return after

    width = PHASES * LANES

    def part_out(n):
        lanes = pl.ds(pl.multiple_of(n * width, width), width)
        return pltpu.make_async_copy(result.at[:, lanes], out.at[:, lanes], out_sems.at[n])

    over_tiles(last, coupled_start(first, TOP, OWN), unroll=4)
    for n in range(TILES // PHASES):
        part_out(n).wait()
    sent.wait()


def finish(count, near_rows, far_rows, got_a, got_b, smooth, w0, w1, w2, tx, ty, tz, k, b):
    rows = 2 * count

    def kernel(*refs):
        finish_kernel(count, *refs)

    return pl.pallas_call(
        kernel,
        out_shape=(
            jax.ShapeDtypeStruct((OWN, PLANE), F32),
            jax.ShapeDtypeStruct((2, LANES), F32),
        )
        + (padded(),) * 9,
        in_specs=in_vmem(13),
        out_specs=tuple(in_hbm(2) + in_vmem(9)),
        input_output_aliases={n + 4: n + 2 for n in range(9)},
        scratch_shapes=[cells(F32), vmem((2, LANES)), semaphores(TILES // PHASES + 1), vmem((count * ALL_ROWS, LANES))]
        + [
            vmem((4, rows + 2 * EDGE, LANES)),
            vmem((3, rows, LANES)),
            vmem((5, rows + 2 * EDGE, LANES)),
            vmem((5, rows, LANES)),
            vmem((5, rows + 2 * EDGE, LANES)),
            vmem((5, rows, LANES)),
        ]
        + [vmem((rows + 2 * EDGE, LANES))] * 5
        + [
            vmem((3, NCY, SPREAD, LANES), BF16),
            vmem((PHASES, 3, NCY, SPREAD, LANES)),
            padded(),
            padded(),
        ]
        + tails(SECOND),
        compiler_params=params(10 + count // 8),
        cost_estimate=lasting(12),
    )(near_rows, far_rows, got_a, got_b, smooth, w0, w1, w2, tx, ty, tz, k, b)[:2]


def swapped(pay_a, pay_b):
    count = lax.axis_size("gx")
    got_a = lax.ppermute(pay_a, "gx", [(i, i ^ 1) for i in range(count)])
    inner = [(i, i + 1 if i % 2 else i - 1) for i in range(1, count - 1)]
    return got_a, lax.ppermute(pay_b, "gx", inner)


def rounds(count):
    bits = count.bit_length() - 1
    found = []
    while bits >= 4:
        low = 1 << (bits - 2)
        found.append((low, 2 * low, 3 * low))
        bits -= 2
    return found + [(1 << bit,) for bit in reversed(range(bits))]


def arrival(count):
    order = [0]
    for steps in rounds(count):
        order = [distance ^ step for step in (0, *steps) for distance in order]
    return order


def stacked_kernel(*refs):
    out, low = refs[-1], 0
    for ref in refs[:-1]:
        out[low : low + ref.shape[0], :] = ref[...]
        low += ref.shape[0]


def stacked(blocks, after=()):
    rows = sum(block.shape[0] for block in blocks)

    def kernel(*refs):
        stacked_kernel(*refs[: len(blocks)], refs[-1])

    return pl.pallas_call(
        kernel,
        out_shape=vmem((rows, LANES)),
        in_specs=in_vmem(len(blocks)) + [pl.BlockSpec(memory_space=pl.ANY)] * len(after),
        out_specs=in_vmem(1)[0],
        compiler_params=params(4),
    )(*blocks, *after)


def gather(rows, after):
    count = lax.axis_size("gx")
    order = rounds(count)
    for n, steps in enumerate(order):
        blocks = [rows]
        for step in steps:
            blocks.append(lax.ppermute(rows, "gx", [(i, i ^ step) for i in range(count)]))
        if steps != (1,):
            rows = stacked(blocks, after if n == len(order) - 2 else ())
    return blocks


def per_device(
    rhs, accumulation, trans_x, trans_y, trans_z, basis_center, basis_side, coarse_inverse
):
    count = lax.axis_size("gx")
    raw, *own_fields, pay_a, pay_b = prepare(
        rhs, accumulation, trans_x, trans_y, trans_z, basis_center, basis_side
    )
    got_a, got_b = swapped(pay_a, pay_b)
    operator = assemble(*own_fields, coarse_inverse)
    *own_fields, k, b, smooth, part, pay_a, pay_b = presmooth(
        got_a, got_b, raw, *own_fields, operator
    )
    got_a, got_b = swapped(pay_a, pay_b)
    near_rows, far_rows = gather(part, (got_a, got_b))
    tx, ty, tz, dg, w0, w1, w2 = own_fields
    return finish(
        count, near_rows, far_rows, got_a, got_b, smooth, w0, w1, w2, tx, ty, tz, k, b
    )


def solution(mesh):
    both = ("grp", "gx")
    cells = P(both, None)
    return jax.shard_map(
        per_device,
        mesh=mesh,
        in_specs=(cells,) * 6 + (P(None, both, None), cells),
        out_specs=(cells, cells),
        check_vma=False,
    )
```

```python
import jax
import jax.numpy as jnp
from jax import lax
from jax.experimental import pallas as pl
from jax.experimental.pallas import tpu as pltpu
from jax.sharding import PartitionSpec as P

BLK = 10
NCY = 8
NCZ = 16
CSW = 6
NZ = 160
PLANE = 12800
COARSE = NCY * NCZ
OMEGA_FINE = 0.7
OMEGA_COARSE = 0.6

LANES = 128
TILES = PLANE // LANES
PHASES = 5
PAIR = 25
PAIRS = TILES // PAIR
OWN = 20
TOP = 3
PAD = OWN + 2 * TOP
HEAD = (TOP, TOP + 1, TOP + 2)
LAST = (TOP + OWN - 1, TOP + OWN - 2, TOP + OWN - 3)
BEFORE = (TOP - 1, TOP - 2, TOP - 3)
BEYOND = (TOP + OWN, TOP + OWN + 1, TOP + OWN + 2)
SPREAD = 32
GROUP = 20
QUARTERS = 4
LT = QUARTERS * NZ // LANES
PAIRED = ((0, 0), (0, 1), (0, 2), (1, 1), (1, 2), (2, 2))
FIRST = 12
SECOND = 15
WHOLE = TILES // 16
REST = TILES % 16
OFFSET = (0, -1, 1)
SAME = ((0, 0), (0, 1), (0, 2), (0, 3), (1, 1), (1, 2), (1, 3), (2, 2), (2, 3), (3, 3), (1, 4), (2, 4), (3, 4))
ACROSS = tuple((u, v) for u in range(4) for v in range(4) if abs(u - v) <= 2)
Y_ROW = len(SAME)
Z_ROW = Y_ROW + len(ACROSS)
INVERSE_ROW = Z_ROW + len(ACROSS)
RHS_ROW = INVERSE_ROW + 1
ALL_ROWS = 48
TAIL = COARSE - NCZ
EDGES = 24
F32 = jnp.float32
BF16 = jnp.bfloat16


def params(mib):
    return pltpu.CompilerParams(vmem_limit_bytes=mib << 20)


def lasting(microseconds):
    return pl.CostEstimate(
        flops=0, transcendentals=0, bytes_accessed=int(3.5e6 * microseconds)
    )


def vmem(shape, dtype=F32):
    return pltpu.VMEM(shape, dtype)


def in_vmem(count):
    return [pl.BlockSpec(memory_space=pltpu.VMEM)] * count


def in_hbm(count):
    return [pl.BlockSpec(memory_space=pltpu.HBM)] * count


def padded():
    return vmem((TILES * PAD + 8, LANES))


def padded_out():
    return pltpu.HBM((TILES * PAD + 8, LANES), F32)


def cells(dtype=BF16):
    return vmem((OWN, PLANE), dtype)


def semaphores(*shape):
    return pltpu.SemaphoreType.DMA(shape)


def stream(sources, buffers, sems):
    width = PLANE // PAIRS

    def copy(field, n):
        lanes = pl.ds(pl.multiple_of(n * width, width), width)
        return pltpu.make_async_copy(
            sources[field].at[..., lanes], buffers[field].at[..., lanes], sems.at[field, n]
        )

    for n in range(PAIRS):
        for field in range(len(sources)):
            copy(field, n).start()

    def wait(n):
        for field in range(len(sources)):
            copy(field, n).wait()

    return wait


def copies(sources, targets, sems):
    made = [
        pltpu.make_async_copy(src, dst, sems.at[n])
        for n, (src, dst) in enumerate(zip(sources, targets))
    ]
    for copy in made:
        copy.start()
    return made


def lane_roll(value, steps):
    return pltpu.roll(value, steps % LANES, 1)


def lanes_of(rows):
    return lax.broadcasted_iota(jnp.int32, (rows, LANES), 1)


def rows_of(rows):
    return lax.broadcasted_iota(jnp.int32, (rows, LANES), 0)


def at(t):
    return pl.ds(pl.multiple_of(t * LANES, LANES), LANES)


def span(t, low, count):
    return pl.ds(t * PAD + low, count)


def own(ref, t):
    return ref[:, at(t)].astype(F32)


def over_tiles(body, carry, before=None, unroll=1):
    def step(n, carry):
        if before is not None:
            before(n)
        for i in range(PAIR):
            carry = body(n * PAIR + i, i, carry)
        return carry

    return lax.fori_loop(0, PAIRS, step, carry, unroll=unroll)


def z_blocks(phase, lane_side):
    cell = lax.broadcasted_iota(jnp.int32, (LANES, LANES), lane_side) + phase * LANES % NZ
    cell = jnp.where(cell >= NZ, cell - NZ, cell)
    first = lax.broadcasted_iota(jnp.int32, (LANES, LANES), 1 - lane_side)
    first = (first % NCZ if lane_side else first) * BLK
    return jnp.where((cell >= first) & (cell < first + BLK), 1.0, 0.0).astype(BF16)


def halves(value):
    high = value.astype(BF16)
    low = (value - high.astype(F32)).astype(BF16)
    return high, low


def remainder(value):
    return value - value.astype(BF16).astype(F32)


def parity():
    return lax.rem(lax.axis_index("gx"), 2)


def coupled(src, tx, ty, tz, t, low, count, carry):
    center, following, turned, y_next, z_flux, y_flux, y_flux_before = carry
    lane = lanes_of(count)
    here = span(t, low, count)
    second = src[span(jnp.minimum(t + 2, TILES - 1), low, count), :]
    turned_next = lane_roll(following, -1)
    z_up = jnp.where(lane == LANES - 1, turned_next, turned)
    y_second = lane_roll(second, -(NZ - LANES))
    y_up = jnp.where(lane >= 2 * LANES - NZ, y_second, y_next)
    tz_t = tz[here, :]
    ty_t = ty[here, :]
    z_flux_new = lane_roll(tz_t * center, 1)
    z_down = jnp.where(lane == 0, z_flux, z_flux_new)
    y_down = jnp.where(lane < NZ - LANES, y_flux_before, y_flux)
    y_flux_new = lane_roll(ty_t * center, NZ - LANES)
    total = tz_t * z_up + z_down
    total = total + (ty_t * y_up + y_down)
    total = total + tx[here, :] * src[span(t, low + 1, count), :]
    total = total + tx[span(t, low - 1, count), :] * src[span(t, low - 1, count), :]
    return total, (following, second, turned_next, y_second, z_flux_new, y_flux_new, y_flux)


def coupled_start(src, low, count):
    center = src[span(0, low, count), :]
    following = src[span(1, low, count), :]
    zero = center * 0.0
    turned = lane_roll(center, -1)
    return center, following, turned, lane_roll(following, -(NZ - LANES)), zero, zero, zero


def sweep(src, dst, tx, ty, tz, k, b, low, count):
    def body(t, i, carry):
        total, after = coupled(src, tx, ty, tz, t, low, count, carry)
        here = span(t, low, count)
        dst[here, :] = b[here, :] + (1.0 - OMEGA_FINE) * carry[0] + k[here, :] * total
        return after

    over_tiles(body, coupled_start(src, low, count), unroll=4)


def plane(ref, row, q, size, stride=PAD):
    return pl.ds(16 * q * stride + row, size, stride)


def read_plane(ref, row, stride=PAD):
    return lambda q, size: ref[plane(ref, row, q, size, stride), :]


def send_both(pay_a, pay_b, tail_a, tail_b, right, left):
    even = parity() == 0
    count = len(right)
    for n in range(count):
        for q in range(WHOLE + 1):
            size = 16 if q < WHOLE else REST
            r, l = right[n](q, size), left[n](q, size)
            a, b = jnp.where(even, r, l), jnp.where(even, l, r)
            if q < WHOLE:
                rows = slice((n * WHOLE + q) * 16, (n * WHOLE + q) * 16 + 16)
                pay_a[rows, :] = a.astype(BF16)
                pay_b[rows, :] = b.astype(BF16)
            else:
                rows = slice(n * REST, n * REST + REST)
                tail_a[rows, :] = a
                tail_b[rows, :] = b
    pay_a[count * WHOLE * 16 :, :] = tail_a[...].astype(BF16)
    pay_b[count * WHOLE * 16 :, :] = tail_b[...].astype(BF16)


def received(count, got_a, got_b, tail_a, tail_b):
    even = parity() == 0
    tail_a[...] = got_a[count * WHOLE * 16 :, :].astype(F32)
    tail_b[...] = got_b[count * WHOLE * 16 :, :].astype(F32)

    def both(n, q):
        if q < WHOLE:
            rows = slice((n * WHOLE + q) * 16, (n * WHOLE + q) * 16 + 16)
            a, b = got_a[rows, :].astype(F32), got_b[rows, :].astype(F32)
        else:
            rows = slice(n * REST, n * REST + REST)
            a, b = tail_a[rows, :], tail_b[rows, :]
        return jnp.where(even, b, a), jnp.where(even, a, b)

    return both


def payload_rows(count):
    return -(-count * TILES // 16) * 16


def payload(count):
    return jax.ShapeDtypeStruct((payload_rows(count), LANES), BF16)


def tails(count):
    return [vmem((payload_rows(count) - count * WHOLE * 16, LANES))] * 2


def low_part(f):
    return lambda q, size: remainder(f(q, size))


def prepare_kernel(
    rhs_in, accum_in, x_in, y_in, z_in, center_in, side_in,
    raw, tx_n, ty_n, tz_n, dg_n, w0_n, w1_n, w2_n, pay_a, pay_b,
    rhs_v, accum_v, x_v, y_v, z_v, center_v, side_v, mixed, tail_a, tail_b, sems,
):
    wait = stream(
        (rhs_in, accum_in, x_in, y_in, z_in, center_in, side_in),
        (rhs_v, accum_v, x_v, y_v, z_v, center_v, side_v),
        sems,
    )
    weights = (w0_n, w1_n, w2_n)
    lane = lanes_of(OWN)

    def load(t, i, carry):
        z_before, y_before, y_second = carry
        w0_n[span(t, TOP, OWN), :] = own(center_v, t)
        for x in range(OWN):
            low = i * 2 * OWN + 2 * x
            mixed[low : low + 2, :] = side_v[x, :, at(t)].astype(F32)
        for n, ref in enumerate((w1_n, w2_n)):
            ref[span(t, TOP, OWN), :] = mixed[pl.ds(i * 2 * OWN + n, OWN, 2), :]
        z_pos = (i * LANES + lane) % NZ
        cells = t * LANES + lane
        here = span(t, TOP, OWN)
        x, y, z = own(x_v, t), own(y_v, t), own(z_v, t)
        y_inner = jnp.where(cells < PLANE - NZ, y, 0.0)
        z_inner = jnp.where(z_pos != NZ - 1, z, 0.0)
        z_rolled = lane_roll(z_inner, 1)
        y_rolled = lane_roll(y_inner, NZ - LANES)
        tx_n[span(t, TOP - 1, 1), :] = jnp.zeros((1, LANES), F32)
        tx_n[here, :] = x
        ty_n[here, :] = y_inner
        tz_n[here, :] = z_inner
        total = own(accum_v, t) + x + tx_n[span(t, TOP - 1, OWN), :]
        total = total + y + jnp.where(lane < NZ - LANES, y_second, y_before)
        total = total + z + jnp.where(lane == 0, z_before, z_rolled)
        dg_n[here, :] = total
        raw[here, :] = rhs_v[:, at(t)]
        return z_rolled, y_rolled, y_before

    zero = lanes_of(OWN).astype(F32) * 0.0
    over_tiles(load, (zero, zero, zero), wait, unroll=4)

    def first_sweep(row):
        r, d = read_plane(raw, row), read_plane(dg_n, row)
        return lambda q, size: OMEGA_FINE * r(q, size) / d(q, size)

    def planes(rows):
        near, second, _ = rows
        r, d = read_plane(raw, near), read_plane(dg_n, near)
        found = [r, low_part(r), d, low_part(d)]
        found += [read_plane(ty_n, near), read_plane(tz_n, near), first_sweep(second)]
        found += [read_plane(tx_n, row) for row in rows[:2]]
        return found + [read_plane(w, near) for w in weights]

    right, left = LAST, HEAD
    send_both(pay_a, pay_b, tail_a, tail_b, planes(right), planes(left))


def prepare(*fields):
    return pl.pallas_call(
        prepare_kernel,
        out_shape=(padded(),) * 8 + (payload(FIRST),) * 2,
        in_specs=in_hbm(7),
        out_specs=tuple(in_vmem(10)),
        scratch_shapes=[cells(F32)]
        + [cells()] * 5
        + [vmem((OWN, 2, PLANE), BF16), vmem((PAIR * 2 * OWN, LANES))]
        + tails(FIRST)
        + [semaphores(7, PAIRS)],
        compiler_params=params(46),
        cost_estimate=lasting(6),
    )(*fields)


def add_share(shares, u, v, value):
    pair = (min(u, v), max(u, v))
    shares[pair] = shares[pair] + value if pair in shares else value


def add_face(shares, u, v, value):
    add_share(shares, u, v, -2.0 * value if u == v else -value)


def presmooth_kernel(
    got_a, got_b, raw, tx_in, ty_in, tz_in, dg_in, w0_in, w1_in, w2_in, after,
    tx, ty, tz, dg, w0, w1, w2,
    k, b, smooth, edges, pay_a, pay_b,
    work, tail_a, tail_b, second_a, second_b,
):
    weights = (w0, w1, w2)
    both = received(FIRST, got_a, got_b, tail_a, tail_b)
    for q in range(WHOLE + 1):
        size = 16 if q < WHOLE else REST

        def put(ref, row, value):
            ref[plane(ref, row, q, size), :] = value

        def get(ref, row):
            return ref[plane(ref, row, q, size), :]

        values = [both(n, q) for n in range(FIRST)]
        left, right = [v[0] for v in values], [v[1] for v in values]
        for got, rows in ((left, BEFORE), (right, BEYOND)):
            put(b, rows[0], got[0] + got[1])
            put(ty, rows[0], got[4])
            put(tz, rows[0], got[5])
            put(b, rows[1], got[6])
            put(tx, rows[0], got[7])
            put(tx, rows[1], got[8])
            for a, w in enumerate(weights):
                put(w, rows[0], got[9 + a])
        tx_before = left[7]
        tx_last = get(tx, LAST[0])
        beyond = right[2] + right[3]
        put(dg, BEFORE[0], left[2] + left[3])
        put(dg, BEYOND[0], jnp.where(beyond > 0.0, beyond + tx_last, 0.0))
        put(dg, HEAD[0], get(dg, HEAD[0]) + tx_before)
        first = [get(w, HEAD[0]) for w in weights]
        last = [get(w, LAST[0]) for w in weights]
        from_next = [right[9 + a] for a in range(3)]
        products = [tx_last * last[a] * from_next[c] for a in range(3) for c in range(3)]
        products += [tx_before * first[a] * first[c] for a, c in PAIRED]
        for n, value in enumerate(products):
            edges[plane(edges, n, q, size, EDGES), :] = value

    def scale(t, i, carry):
        here = span(t, TOP - 1, OWN + 2)
        for row in (TOP - 1, TOP + OWN):
            smooth[span(t, row, 1), :] = jnp.zeros((1, LANES), F32)
        diag = dg[here, :]
        value = jnp.where(diag > 0.0, OMEGA_FINE / diag, 0.0)
        k[here, :] = value
        b[span(t, TOP, OWN), :] = raw[span(t, TOP, OWN), :]
        b[here, :] = value * b[here, :]
        return carry

    over_tiles(scale, 0, unroll=4)
    sweep(b, work, tx, ty, tz, k, b, TOP - 1, OWN + 2)
    sweep(work, smooth, tx, ty, tz, k, b, TOP, OWN)
    for q in range(WHOLE + 1):
        size = 16 if q < WHOLE else REST
        last = tx[plane(tx, LAST[0], q, size), :] * smooth[plane(smooth, LAST[0], q, size), :]
        first = tx[plane(tx, BEFORE[0], q, size), :] * smooth[plane(smooth, HEAD[0], q, size), :]
        values = [last * w[plane(w, BEYOND[0], q, size), :] for w in weights]
        values += [first * w[plane(w, BEFORE[0], q, size), :] for w in weights]
        values += [jnp.zeros((size, LANES), F32)] * 3
        for n, value in enumerate(values):
            edges[plane(edges, 15 + n, q, size, EDGES), :] = value

    def planes(rows):
        near = read_plane(smooth, rows[0])
        found = [near, low_part(near), read_plane(smooth, rows[1]), read_plane(smooth, rows[2])]
        found += [read_plane(w, row) for w in weights for row in rows[1:]]
        found += [read_plane(ref, rows[1]) for ref in (raw, dg, ty, tz)]
        return found + [read_plane(tx, rows[2])]

    send_both(pay_a, pay_b, second_a, second_b, planes(LAST), planes(HEAD))


def presmooth(got_a, got_b, raw, tx, ty, tz, dg, w0, w1, w2, operator):
    return pl.pallas_call(
        presmooth_kernel,
        out_shape=(padded(),) * 10 + (vmem((TILES * EDGES, LANES)),) + (payload(SECOND),) * 2,
        in_specs=in_vmem(11),
        out_specs=tuple(in_vmem(13)),
        input_output_aliases={n + 3: n for n in range(7)},
        scratch_shapes=[padded()] + tails(FIRST) + tails(SECOND),
        compiler_params=params(8),
        cost_estimate=lasting(4),
    )(got_a, got_b, raw, tx, ty, tz, dg, w0, w1, w2, operator)


def restrict_kernel(
    smooth, raw, tx, ty, tz, dg, w0, w1, w2, edges, operator, part, sums, rest, shares_v
):
    weights = (w0, w1, w2)
    rows = 48 + EDGES
    lane = lanes_of(rows)
    row8 = rows_of(8)
    for n in range(PAIR):
        rest[n * 24 + 16 : n * 24 + 24, :] = jnp.zeros((8, LANES), F32)

    def residual(t, i, carry):
        total, following = coupled(smooth, tx, ty, tz, t, TOP, OWN, carry)
        rest[i * 24 : i * 24 + OWN, :] = (
            raw[span(t, TOP, OWN), :] - dg[span(t, TOP, OWN), :] * carry[0] + total
        )
        left_over = rest[i * 24 : i * 24 + 24, :]
        folded = []
        for w in weights:
            f = w[span(t, TOP, 24), :] * left_over
            mixed = jnp.where(row8 < BLK - 8, f[8:16], 0.0)
            folded += [f[0:8] + mixed, jnp.where(row8 < 4, f[16:24], 0.0) + (f[8:16] - mixed)]
        for n, value in enumerate(folded):
            shares_v[pl.ds(t * rows + 8 * n, 8), :] = value
        shares_v[pl.ds(t * rows + 48, EDGES), :] = edges[pl.ds(t * EDGES, EDGES), :]
        return following

    over_tiles(residual, coupled_start(smooth, TOP, OWN), unroll=4)

    def strips(n, carry):
        for strip in range(2):
            for phase in range(PHASES):
                total = None
                for i in range(phase, PAIR, PHASES):
                    if strip == 0 and i > PAIR // 2 or strip == 1 and i < PAIR // 2:
                        continue
                    value = shares_v[pl.ds((n * PAIR + i) * rows, rows), :]
                    if i == PAIR // 2:
                        value = jnp.where((lane < LANES // 2) == (strip == 0), value, 0.0)
                    total = value if total is None else total + value
                sums[phase, 2 * n + strip] = total
        return carry

    lax.fori_loop(0, PAIRS, strips, 0)

    found = jnp.zeros((NCY * (48 + EDGES), LANES), F32)
    for phase in range(PHASES):
        pick = z_blocks(phase, 0)
        pieces = halves(sums[phase].reshape(NCY * (48 + EDGES), LANES))
        found = found + jnp.dot(
            jnp.concatenate(pieces, axis=1),
            jnp.concatenate([pick, pick], axis=0),
            preferred_element_type=F32,
        )
    placed = found[0:rows]
    for strip in range(1, NCY):
        placed = placed + lane_roll(found[strip * rows : strip * rows + rows], strip * NCZ)
    shares = {}
    for n, (a, c) in enumerate(PAIRED):
        add_share(shares, 1 + OFFSET[a], 1 + OFFSET[c], placed[57 + n : 58 + n])
    for a in range(3):
        for c in range(3):
            add_face(shares, 2 + OFFSET[a], 3 + OFFSET[c], placed[48 + 3 * a + c : 49 + 3 * a + c])
    part[0:ALL_ROWS, :] = operator[...]
    for n, pair in enumerate(SAME):
        if pair in shares:
            part[n : n + 1, :] += shares[pair]
    for a in range(3):
        for block in range(2):
            row = RHS_ROW + 2 + block + OFFSET[a]
            low = (2 * a + block) * 8
            part[row : row + 1, :] += jnp.sum(placed[low : low + 8], axis=0, keepdims=True)
        for low, u in ((63, 3), (66, 0)):
            row = RHS_ROW + 1 + u + OFFSET[a]
            part[row : row + 1, :] += placed[low + a : low + a + 1]


def restrict(smooth, raw, tx, ty, tz, dg, w0, w1, w2, edges, operator):
    return pl.pallas_call(
        restrict_kernel,
        out_shape=vmem((ALL_ROWS, LANES)),
        in_specs=in_vmem(11),
        out_specs=in_vmem(1)[0],
        scratch_shapes=[
            vmem((PHASES, NCY, 48 + EDGES, LANES)),
            vmem((PAIR * 24, LANES)),
            vmem((TILES * (48 + EDGES), LANES)),
        ],
        compiler_params=params(10),
        cost_estimate=lasting(3),
    )(smooth, raw, tx, ty, tz, dg, w0, w1, w2, edges, operator)


def regrouped(ref, dst, shift, index, load, cut=False):
    lane = lanes_of(OWN)
    rolled = {}

    def piece(quarter, t):
        offset = 3200 * quarter + NZ * shift - NZ * quarter
        first, turn = (t * LANES + offset) // LANES, offset % LANES

        def source(tile):
            tile = min(max(tile, 0), TILES - 1)
            key = (tile, turn)
            if key not in rolled:
                value = load(ref, tile)
                rolled[key] = lane_roll(value, -turn) if turn else value
            return rolled[key]

        if quarter * GROUP + shift < 0 or quarter * GROUP + shift >= 4 * GROUP:
            return None
        low_lane, high_lane = max(0, quarter * NZ - t * LANES), min(LANES, (quarter + 1) * NZ - t * LANES)
        if turn == 0 or high_lane <= LANES - turn:
            return source(first)
        if low_lane >= LANES - turn:
            return source(first + 1)
        return jnp.where(lane < LANES - turn, source(first), source(first + 1))

    for t in range(LT):
        first = t * LANES // NZ
        last = (t * LANES + LANES - 1) // NZ
        value = piece(first, t)
        if last != first:
            other = piece(last, t)
            value = jnp.zeros((OWN, LANES), F32) if value is None else value
            other = jnp.zeros((OWN, LANES), F32) if other is None else other
            value = jnp.where(lane < last * NZ - t * LANES, value, other)
        elif value is None:
            value = jnp.zeros((OWN, LANES), F32)
        if cut:
            value = jnp.where(rows_of(OWN) < OWN - 1, value, 0.0)
        dst[index, t, 0:OWN, :] = value
        if index >= BLK:
            dst[index - BLK, t, OWN : OWN + 4, :] = value[16:OWN]
        else:
            dst[index, t, 24:SPREAD, :] = jnp.zeros((SPREAD - 24, LANES), F32)


def assemble_kernel(
    tx_n, ty_n, tz_n, dg_n, w0_n, w1_n, w2_n, inverse, out,
    w, tx, ty, tz, dg, fields, rows_in, found,
):
    weights = (w0_n, w1_n, w2_n)

    def plain(ref, tile):
        return ref[tile * PAD + TOP : tile * PAD + TOP + OWN, :]

    for g in range(GROUP):
        regrouped(tx_n, tx, g, g, plain, cut=True)
        regrouped(ty_n, ty, g, g, plain)
        regrouped(tz_n, tz, g, g, plain)
        regrouped(dg_n, dg, g, g, plain)
    for g in range(GROUP + 1):
        for a, weight in enumerate(weights):
            regrouped(weight, w.at[a], g, g, plain)

    lane8 = lanes_of(8)

    def combo(index, carry):
        shared = index >= 4 * LT
        half = jnp.where(shared, 0, index // (2 * LT))
        t = jnp.where(shared, index - 4 * LT, index // 2 % LT)
        low = jnp.where(shared, 16, index % 2 * 8)
        t_next = jnp.minimum(t + 1, LT - 1)
        same = pl.ds(pl.multiple_of(low, 8), 8)
        after = pl.ds(low + 1, 8)
        d_sum = [None] * 6
        x_sum = [None] * 9
        z_sum = [None] * 9
        for step in range(BLK):
            g = half * BLK + step
            here = [w[a, g, t, same, :] for a in range(3)]
            x_up = [w[a, g, t, after, :] for a in range(3)]
            y_up = [w[a, g + 1, t, same, :] for a in range(3)]
            z_up = [
                jnp.where(
                    lane8 == LANES - 1,
                    lane_roll(w[a, g, t_next, same, :], -1),
                    lane_roll(here[a], -1),
                )
                for a in range(3)
            ]
            d_t, x_t = dg[g, t, same, :], tx[g, t, same, :]
            y_t, z_t = ty[g, t, same, :], tz[g, t, same, :]
            d_w = [d_t * v for v in here]
            x_w = [x_t * v for v in here]
            y_w = [y_t * v for v in here]
            z_w = [z_t * v for v in here]
            for n, (a, c) in enumerate(PAIRED):
                term = d_w[a] * here[c]
                if step < BLK - 1:
                    cross = y_w[a] * y_up[c]
                    cross = cross + (cross if a == c else y_w[c] * y_up[a])
                    term = term - cross
                d_sum[n] = term if d_sum[n] is None else d_sum[n] + term
            for a in range(3):
                for c in range(3):
                    n = 3 * a + c
                    x_term = x_w[a] * x_up[c]
                    z_term = z_w[a] * z_up[c]
                    x_sum[n] = x_term if x_sum[n] is None else x_sum[n] + x_term
                    z_sum[n] = z_term if z_sum[n] is None else z_sum[n] + z_term
                    if step == BLK - 1:
                        fields[24 + n, half, t, same, :] = y_w[a] * y_up[c]
        for n in range(6):
            fields[n, half, t, same, :] = d_sum[n]
        for n in range(9):
            fields[6 + n, half, t, same, :] = x_sum[n]
            fields[15 + n, half, t, same, :] = z_sum[n]
        return carry

    lax.fori_loop(0, 5 * LT, combo, 0)

    row8 = rows_of(8)

    def fold(index, carry):
        half = index // LT
        t = index % LT
        cols = pl.ds(pl.multiple_of(half * LANES, LANES), LANES)

        mine = (row8 < 4) == (half == 0)

        def tiles_of(n):
            found = [fields[n, half, t, 8 * s : 8 * s + 8, :] for s in range(2)]
            return found + [jnp.where(mine, fields[n, 0, t, 16:24, :], 0.0)]

        def blocks(v, first):
            return (
                v[0] + jnp.where(row8 < first, v[1], 0.0),
                jnp.where(row8 >= 2, v[1], 0.0) + v[2],
            )

        x_tiles = [tiles_of(6 + n) for n in range(9)]
        x_in = [blocks(v, 1) for v in x_tiles]
        for n, (a, c) in enumerate(PAIRED):
            both = blocks(tiles_of(n), 2)
            for s in range(2):
                value = both[s] - x_in[3 * a + c][s] - x_in[3 * c + a][s]
                rows_in[t, 16 * n + 8 * s : 16 * n + 8 * s + 8, cols] = value
        for n in range(9):
            rows_in[t, 96 + 8 * n : 104 + 8 * n, cols] = jnp.where(row8 == 1, x_tiles[n][1], 0.0)
            for first, base in ((24, 168), (15, 312)):
                both = blocks(tiles_of(first + n), 2)
                for s in range(2):
                    low = base + 16 * n + 8 * s
                    rows_in[t, low : low + 8, cols] = both[s]
        return carry

    lax.fori_loop(0, 2 * LT, fold, 0)

    coarse = lanes_of(8)
    first = coarse // (2 * NCZ) * NZ + coarse % NCZ * BLK
    first = jnp.concatenate(
        [jnp.where(coarse // NCZ % 2 == half, first, -NZ) for half in range(2) for _ in range(NCZ)],
        axis=0,
    )
    place = jnp.concatenate([rows_of(LANES)] * 2, axis=0)
    total = jnp.zeros((456, 2 * LANES), F32)
    for t in range(LT):
        step = place + t * LANES - first
        inside = jnp.where((step >= 0) & (step < BLK - 1), 1.0, 0.0)
        crossing = jnp.where(step == BLK - 1, 1.0, 0.0)
        pick = jnp.concatenate([inside, crossing], axis=1).astype(BF16)
        for piece in halves(rows_in[t]):
            total = total + jnp.dot(piece, pick, preferred_element_type=F32)
    found[0:57, :] = jnp.sum(total.reshape(57, 8, 2 * LANES), axis=1)

    def both(row):
        return found[row : row + 1, 0:LANES] + found[row : row + 1, LANES:]

    def inside(row):
        return found[row : row + 1, 0:LANES]

    def crossing(row):
        return found[row : row + 1, LANES:]

    shares, y_shares, z_shares = {}, {}, {}
    for block in range(2):
        rows = [1 + block + OFFSET[a] for a in range(3)]
        for n, (a, c) in enumerate(PAIRED):
            value = both(2 * n + block)
            value = value - inside(39 + 2 * (3 * a + c) + block) - inside(39 + 2 * (3 * c + a) + block)
            add_share(shares, rows[a], rows[c], value)
        for a in range(3):
            for c in range(3):
                n = 3 * a + c
                pair = (rows[a], rows[c])
                for kept, value in (
                    (y_shares, both(21 + 2 * n + block)),
                    (z_shares, crossing(39 + 2 * n + block)),
                ):
                    kept[pair] = kept[pair] - value if pair in kept else -value
                if block == 0:
                    add_face(shares, 1 + OFFSET[a], 2 + OFFSET[c], both(12 + n))
    out[...] = jnp.zeros_like(out)
    for first, pairs, kept in ((0, SAME, shares), (Y_ROW, ACROSS, y_shares), (Z_ROW, ACROSS, z_shares)):
        for n, pair in enumerate(pairs):
            if pair in kept:
                out[first + n : first + n + 1, :] = kept[pair]
    out[INVERSE_ROW : INVERSE_ROW + 1, :] = inverse[0:1, :]
    lane = lanes_of(1)
    for n in range(NCY):
        row = Y_ROW + n
        moved = lane_roll(inverse[1:2, :], TAIL - n * NCZ)
        out[row : row + 1, :] = jnp.where(lane < TAIL, out[row : row + 1, :], moved)


def assemble(tx, ty, tz, dg, w0, w1, w2, inverse):
    slab = (LT, SPREAD, LANES)
    return pl.pallas_call(
        assemble_kernel,
        out_shape=vmem((ALL_ROWS, LANES)),
        in_specs=in_vmem(8),
        out_specs=in_vmem(1)[0],
        scratch_shapes=[
            vmem((3, GROUP + 1) + slab),
            vmem((GROUP,) + slab),
            vmem((GROUP,) + slab),
            vmem((GROUP,) + slab),
            vmem((GROUP,) + slab),
            vmem((33, 2, LT, 24, LANES)),
            vmem((LT, 456, 2 * LANES)),
            vmem((57, 2 * LANES)),
        ],
        compiler_params=params(24),
        cost_estimate=lasting(10),
    )(tx, ty, tz, dg, w0, w1, w2, inverse)


EDGE = 8


def coarse_solve(count, halves_in, gathered, same, same_t, y_mat, y_mat_t, z_mat, z_mat_t, inv, rhs, e, e_y, e_z):
    rows = 2 * count
    here = pl.ds(EDGE, rows)
    for ref in (same, y_mat, z_mat, inv, rhs, e, e_y, e_z):
        ref[...] = jnp.zeros_like(ref)
    index = lax.axis_index("gx")
    for n, distance in enumerate(arrival(count)):
        ref, n = halves_in[n // (count // 2)], n % (count // 2)
        place = pl.multiple_of(lax.bitwise_xor(index, distance) * ALL_ROWS, ALL_ROWS)
        gathered[pl.ds(place, ALL_ROWS), :] = ref[n * ALL_ROWS : n * ALL_ROWS + ALL_ROWS, :]

    def share(row):
        return gathered[pl.ds(row, count, ALL_ROWS), :]

    def add(ref, u, value):
        place = pl.ds(EDGE - 1 + u, count, 2)
        ref[place, :] = ref[place, :] + value

    for n, (u, v) in enumerate(SAME):
        add(same.at[v - u], u, share(n))
    lane = lanes_of(count)
    second = jnp.zeros((count, LANES), F32)
    for n, (u, v) in enumerate(ACROSS):
        value = share(Y_ROW + n)
        add(y_mat.at[v - u + 2], u, jnp.where(lane < TAIL, value, 0.0))
        if n < NCY:
            moved = lane_roll(value, n * NCZ - TAIL)
            second = jnp.where((lane >= n * NCZ) & (lane < n * NCZ + NCZ), moved, second)
        add(z_mat.at[v - u + 2], u, share(Z_ROW + n))
    for u in range(-1, 5):
        add(rhs, u, share(RHS_ROW + 1 + u))
    inv[pl.ds(EDGE, count, 2), :] = OMEGA_COARSE * share(INVERSE_ROW)
    inv[pl.ds(EDGE + 1, count, 2), :] = OMEGA_COARSE * second
    for step in range(1, 4):
        same_t[step - 1] = same[step, pl.ds(EDGE - step, rows), :]
    for step in range(-2, 3):
        y_mat_t[step + 2] = y_mat[step + 2, pl.ds(EDGE - step, rows), :]
        z_mat_t[step + 2] = z_mat[step + 2, pl.ds(EDGE - step, rows), :]
    e[here, :] = inv[here, :] * rhs[here, :]

    def one(index, carry):
        at_step = {step: e[pl.ds(EDGE + step, rows), :] for step in range(-3, 4)}
        e_y[here, :] = lane_roll(at_step[0], -NCZ)
        e_z[here, :] = lane_roll(at_step[0], -1)
        image = same[0, here, :] * at_step[0]
        for step in range(1, 4):
            image = image + same[step, here, :] * at_step[step] + same_t[step - 1] * at_step[-step]
        y_back = z_back = None
        for step in range(-2, 3):
            y_term = y_mat_t[step + 2] * at_step[-step]
            z_term = z_mat_t[step + 2] * at_step[-step]
            y_back = y_term if y_back is None else y_back + y_term
            z_back = z_term if z_back is None else z_back + z_term
        image = image + lane_roll(y_back, NCZ) + lane_roll(z_back, 1)
        for step in range(-2, 3):
            place = pl.ds(EDGE + step, rows)
            image = image + y_mat[step + 2, here, :] * e_y[place, :]
            image = image + z_mat[step + 2, here, :] * e_z[place, :]
        e[here, :] = at_step[0] + inv[here, :] * (rhs[here, :] - image)
        return carry

    lax.fori_loop(0, CSW - 1, one, 0)


def finish_kernel(
    count, near_rows, far_rows, got_a, got_b,
    smooth_in, w0_in, w1_in, w2_in, tx_in, ty_in, tz_in, k_in, b_in,
    out, update, smooth, w0, w1, w2, tx, ty, tz, k, b,
    result, own_update, out_sems, gathered, same, same_t, y_mat, y_mat_t, z_mat, z_mat_t, inv, rhs, e, e_y, e_z, strips, spread, first, second, tail_a, tail_b,
):
    weights = (w0, w1, w2)
    coarse_solve(
        count, (near_rows, far_rows), gathered, same, same_t, y_mat, y_mat_t, z_mat, z_mat_t, inv, rhs, e, e_y, e_z
    )
    base = EDGE + 2 * lax.axis_index("gx")
    own_update[...] = e[pl.ds(base, 2), :]
    sent = pltpu.make_async_copy(own_update, update, out_sems.at[TILES // PHASES])
    sent.start()
    near = {s: e[pl.ds(base + s, 1), :] for s in range(-2, 4)}
    row = rows_of(SPREAD)
    lane = lanes_of(SPREAD)
    for a, s in enumerate((0, -1, 1)):
        value = jnp.where(row < TOP + BLK, near[s], near[s + 1])
        value = jnp.where(row < TOP, near[s - 1], value)
        value = jnp.where(row >= TOP + OWN, near[s + 2], value)
        high = value.astype(BF16).astype(F32)
        rest = value - high
        low = rest.astype(BF16).astype(F32)
        rest = rest - low
        for strip in range(NCY):
            turned = lane_roll(high, -strip * NCZ)
            turned = jnp.where(lane < NCZ, turned, lane_roll(low, (1 - strip) * NCZ))
            turned = jnp.where(lane < 2 * NCZ, turned, lane_roll(rest, (2 - strip) * NCZ))
            turned = jnp.where(lane < 3 * NCZ, turned, 0.0)
            strips[a, strip] = turned.astype(BF16)
    flat = strips[...].reshape(3 * NCY * SPREAD, LANES)
    for phase in range(PHASES):
        pick = z_blocks(phase, 1)
        got = jnp.dot(flat, pick, preferred_element_type=F32)
        spread[phase] = got.reshape(3, NCY, SPREAD, LANES)

    both = received(SECOND, got_a, got_b, tail_a, tail_b)
    for q in range(WHOLE + 1):
        size = 16 if q < WHOLE else REST
        values = [both(n, q) for n in range(SECOND)]
        for side, rows in ((0, BEFORE), (1, BEYOND)):
            got = [v[side] for v in values]
            for row, value in zip(rows, (got[0] + got[1], got[2], got[3])):
                smooth[plane(smooth, row, q, size), :] = value
            for a, w in enumerate(weights):
                for n, row in enumerate(rows[1:]):
                    w[plane(w, row, q, size), :] = got[4 + 2 * a + n]
            scale = jnp.where(got[11] > 0.0, OMEGA_FINE / got[11], 0.0)
            for ref, value in ((k, scale), (b, scale * got[10]), (ty, got[12]), (tz, got[13])):
                ref[plane(ref, rows[1], q, size), :] = value
            if side == 0:
                tx[plane(tx, rows[2], q, size), :] = got[14]

    def prolong(t, i, carry):
        n = t // PAIR
        phase = i % PHASES
        here = span(t, 0, PAD)
        total = smooth[here, :]
        for a, w in enumerate(weights):
            if i == PAIR // 2:
                values = jnp.where(
                    lane[0:PAD] < LANES // 2,
                    spread[phase, a, 2 * n, 0:PAD],
                    spread[phase, a, 2 * n + 1, 0:PAD],
                )
            else:
                values = spread[phase, a, 2 * n + (1 if i > PAIR // 2 else 0), 0:PAD]
            total = total + w[here, :] * values
        first[here, :] = total
        return carry

    over_tiles(prolong, 0)
    sweep(first, second, tx, ty, tz, k, b, TOP - 2, OWN + 4)
    sweep(second, first, tx, ty, tz, k, b, TOP - 1, OWN + 2)

    def last(t, i, carry):
        total, after = coupled(first, tx, ty, tz, t, TOP, OWN, carry)
        here = span(t, TOP, OWN)
        result[:, at(t)] = b[here, :] + (1.0 - OMEGA_FINE) * carry[0] + k[here, :] * total
        if i % PHASES == PHASES - 1:
            part_out(t // PHASES).start()
        return after

    width = PHASES * LANES

    def part_out(n):
        lanes = pl.ds(pl.multiple_of(n * width, width), width)
        return pltpu.make_async_copy(result.at[:, lanes], out.at[:, lanes], out_sems.at[n])

    over_tiles(last, coupled_start(first, TOP, OWN), unroll=4)
    for n in range(TILES // PHASES):
        part_out(n).wait()
    sent.wait()


def finish(count, near_rows, far_rows, got_a, got_b, smooth, w0, w1, w2, tx, ty, tz, k, b):
    rows = 2 * count

    def kernel(*refs):
        finish_kernel(count, *refs)

    return pl.pallas_call(
        kernel,
        out_shape=(
            jax.ShapeDtypeStruct((OWN, PLANE), F32),
            jax.ShapeDtypeStruct((2, LANES), F32),
        )
        + (padded(),) * 9,
        in_specs=in_vmem(13),
        out_specs=tuple(in_hbm(2) + in_vmem(9)),
        input_output_aliases={n + 4: n + 2 for n in range(9)},
        scratch_shapes=[cells(F32), vmem((2, LANES)), semaphores(TILES // PHASES + 1), vmem((count * ALL_ROWS, LANES))]
        + [
            vmem((4, rows + 2 * EDGE, LANES)),
            vmem((3, rows, LANES)),
            vmem((5, rows + 2 * EDGE, LANES)),
            vmem((5, rows, LANES)),
            vmem((5, rows + 2 * EDGE, LANES)),
            vmem((5, rows, LANES)),
        ]
        + [vmem((rows + 2 * EDGE, LANES))] * 5
        + [
            vmem((3, NCY, SPREAD, LANES), BF16),
            vmem((PHASES, 3, NCY, SPREAD, LANES)),
            padded(),
            padded(),
        ]
        + tails(SECOND),
        compiler_params=params(10 + count // 8),
        cost_estimate=lasting(12),
    )(near_rows, far_rows, got_a, got_b, smooth, w0, w1, w2, tx, ty, tz, k, b)[:2]


def swapped(pay_a, pay_b):
    count = lax.axis_size("gx")
    got_a = lax.ppermute(pay_a, "gx", [(i, i ^ 1) for i in range(count)])
    inner = [(i, i + 1 if i % 2 else i - 1) for i in range(1, count - 1)]
    return got_a, lax.ppermute(pay_b, "gx", inner)


def rounds(count):
    bits = count.bit_length() - 1
    found = []
    while bits >= 4:
        low = 1 << (bits - 2)
        found.append((low, 2 * low, 3 * low))
        bits -= 2
    return found + [(1 << bit,) for bit in reversed(range(bits))]


def arrival(count):
    order = [0]
    for steps in rounds(count):
        order = [distance ^ step for step in (0, *steps) for distance in order]
    return order


def stacked_kernel(*refs):
    out, low = refs[-1], 0
    for ref in refs[:-1]:
        out[low : low + ref.shape[0], :] = ref[...]
        low += ref.shape[0]


def stacked(blocks, after=()):
    rows = sum(block.shape[0] for block in blocks)

    def kernel(*refs):
        stacked_kernel(*refs[: len(blocks)], refs[-1])

    return pl.pallas_call(
        kernel,
        out_shape=vmem((rows, LANES)),
        in_specs=in_vmem(len(blocks)) + [pl.BlockSpec(memory_space=pl.ANY)] * len(after),
        out_specs=in_vmem(1)[0],
        compiler_params=params(4),
    )(*blocks, *after)


def gather(rows, after):
    count = lax.axis_size("gx")
    order = rounds(count)
    for n, steps in enumerate(order):
        blocks = [rows]
        for step in steps:
            blocks.append(lax.ppermute(rows, "gx", [(i, i ^ step) for i in range(count)]))
        if steps != (1,):
            rows = stacked(blocks, after if n == len(order) - 2 else ())
    return blocks


def per_device(
    rhs, accumulation, trans_x, trans_y, trans_z, basis_center, basis_side, coarse_inverse
):
    count = lax.axis_size("gx")
    raw, *own_fields, pay_a, pay_b = prepare(
        rhs, accumulation, trans_x, trans_y, trans_z, basis_center,
        basis_side.transpose(1, 0, 2),
    )
    got_a, got_b = swapped(pay_a, pay_b)
    operator = assemble(*own_fields, coarse_inverse)
    *own_fields, k, b, smooth, edges, pay_a, pay_b = presmooth(
        got_a, got_b, raw, *own_fields, operator
    )
    got_a, got_b = swapped(pay_a, pay_b)
    part = restrict(smooth, raw, *own_fields, edges, operator)
    near_rows, far_rows = gather(part, (got_a, got_b))
    tx, ty, tz, dg, w0, w1, w2 = own_fields
    return finish(
        count, near_rows, far_rows, got_a, got_b, smooth, w0, w1, w2, tx, ty, tz, k, b
    )


def solution(mesh):
    both = ("grp", "gx")
    cells = P(both, None)
    return jax.shard_map(
        per_device,
        mesh=mesh,
        in_specs=(cells,) * 6 + (P(None, both, None), cells),
        out_specs=(cells, cells),
        check_vma=False,
    )
```
